32 devices in a mesh: groups: 2 (over x), row: 16 (over z, y, core).
Axes of the slice: x: 2, y: 2, z: 4, core: 2. Of those that a mesh axis runs over, the one named last changes fastest.
Arguments:
- alignment_input: bfloat16 [64, 256, 64], P('groups', 'row'), parts along dimension 0, may hold values from -6 to 6
- alignment_mask: int32 [64, 256], P('groups'), parts along dimension 0, may hold values from 0 to 1, as said below
- residue_mask: int32 [512], P('groups'), parts along dimension 0, may hold values 0 or 1
- left_weight: bfloat16 [64, 32], replicated, may hold values from -0.75 to 0.75
- right_weight: bfloat16 [64, 32], replicated, may hold values from -0.75 to 0.75
- output_weight: bfloat16 [1024, 128], replicated, may hold values from -0.1875 to 0.1875
- pairwise_gradient: bfloat16 [512, 256, 128], P(('groups', 'row')), parts along dimension 0, may hold values from -6 to 6
Outputs:
- msa_grad: float32 [64, 256, 64], P('groups', 'row'), parts along dimension 0
The draws below stay inside these ranges and needn't reach their ends.
There are 2 independent parts, one for each index of `groups`. The reference program is written for one: setup_inputs(seed, part) draws one part's arguments, and reference() takes and returns one part's arrays. A program takes and returns all parts, laid end to end along the dimension named above; an argument that names none is the same for every part. Nothing has to cross between parts.
Inputs may be any that keep to these rules, and one draw needn't show every extreme that they name: `alignment_mask`: sequence 0 is present at every residue.
All inputs are finite; a program needn't handle non-finite values.
Results may differ from the reference program's by a relative error of at most 0.005.
Values may be sent and summed in bfloat16 or wider, within the bound.
No kernel may reach another device: no remote copies, remote signals or barrier semaphores. Data moves between devices by JAX's collectives and lax.ppermute only.
A program may use at most 128 MiB of HBM per device.

```python
import jax
import jax.numpy as jnp
from jax import lax

ALIGN_FEATURES = 64
HIDDEN_CHANNELS = 32
C_PAIR = 128
NI = 16
SEQUENCE_COUNT = 32
RESIDUE_COUNT = 256
CP = 1024


def draw_alignment_mask(key, part):
    key = jax.random.fold_in(key, 11)
    level_key, roll_key = jax.random.split(key)
    levels = jax.random.randint(level_key, (SEQUENCE_COUNT, 1), 2, 9)
    rolls = jax.random.randint(roll_key, (SEQUENCE_COUNT, RESIDUE_COUNT), 0, 8)
    present = (rolls < levels).astype(jnp.int32)
    first = jnp.arange(SEQUENCE_COUNT, dtype=jnp.int32)[:, None] == 0
    return jnp.where(first, jnp.ones((SEQUENCE_COUNT, RESIDUE_COUNT), jnp.int32), present).astype(jnp.int32)


def set_ends(drawn, stream_key, smallest, top_value):
    longest = drawn.shape.index(max(drawn.shape))
    spots = []
    for shift in (0, 1):
        where = [jax.random.randint(jax.random.fold_in(stream_key, axis), (), 0, length) for axis, length in enumerate(drawn.shape)]
        where[longest] = (where[longest] + shift) % drawn.shape[longest]
        spots.append(tuple(where))
    return drawn.at[spots[0]].set(smallest).at[spots[1]].set(top_value)


def block_levels(rng, shape, shards, low, top_value):
    gain = 1.0
    for position, blocks in shards:
        draws = jax.random.uniform(jax.random.fold_in(jax.random.fold_in(rng, 6), position), (blocks,), jnp.float32, low / len(shards), top_value / len(shards))
        gain = gain * jnp.repeat(jnp.exp(draws), shape[position] // blocks).reshape((-1,) + (1,) * (len(shape) - 1 - position))
    return gain


def noise(stream_key, extent, scale, most, shards=(), held_as=jnp.bfloat16):
    array = jax.random.normal(stream_key, extent, jnp.float32) * scale
    if len(shards) > 0:
        array = block_levels(stream_key, extent, shards, -0.22, 0.18) * array
    return jnp.clip(array, min=-most, max=most).astype(held_as)


def setup_inputs(seed: int = 0, part: int = 0) -> dict:
    keys = jax.random.split(jax.random.key(seed), 8)
    own_keys = jax.random.split(jax.random.fold_in(keys[7], part), 8)
    return {
        "alignment_input": noise(own_keys[0], (SEQUENCE_COUNT, RESIDUE_COUNT, ALIGN_FEATURES), 1.0, 6.0, ((1, 16),)),
        "alignment_mask": draw_alignment_mask(jax.random.fold_in(jax.random.fold_in(keys[7], part), 71), part),
        "residue_mask": set_ends((jax.random.randint(own_keys[2], (RESIDUE_COUNT,), 0, 8) < 7).astype(jnp.int32), jax.random.fold_in(own_keys[2], 1), 0, 1),
        "left_weight": noise(keys[3], (ALIGN_FEATURES, HIDDEN_CHANNELS), ALIGN_FEATURES ** -0.5, 0.75),
        "right_weight": noise(keys[4], (ALIGN_FEATURES, HIDDEN_CHANNELS), ALIGN_FEATURES ** -0.5, 0.75),
        "output_weight": noise(keys[5], (CP, C_PAIR), CP ** -0.5, 0.1875),
        "pairwise_gradient": noise(own_keys[6], (RESIDUE_COUNT, RESIDUE_COUNT, C_PAIR), 1.0, 6.0, ((0, 16),)),
    }


def layer_normalize(alignment_input):
    value_rows = alignment_input.astype(jnp.float32)
    centered = value_rows - lax.optimization_barrier(jnp.mean(value_rows, axis=-1, keepdims=True))
    inverse_deviation = lax.rsqrt(lax.optimization_barrier(jnp.mean(centered * centered, axis=-1, keepdims=True)) + 1e-05)
    return (centered * inverse_deviation, inverse_deviation)

def project(normalized_input, weight, presence_mask):
    feature_depth, width, channels = normalized_input.shape
    normed_half = normalized_input.astype(jnp.bfloat16)
    flat = jnp.dot(normed_half.reshape(feature_depth * width, channels), weight, preferred_element_type=jnp.float32)
    return (presence_mask[:, :, None] * flat.reshape(feature_depth, width, weight.shape[1])).astype(jnp.bfloat16)

def tile_grad(grad_tile, norm_tile, output_weight):
    first, second, width = grad_tile.shape
    flat = jnp.dot(grad_tile.reshape(first * second, width), output_weight.T, preferred_element_type=jnp.float32)
    scaled = flat.reshape(first, second, HIDDEN_CHANNELS, HIDDEN_CHANNELS) / norm_tile[:, :, None, None]
    return scaled.astype(jnp.bfloat16)

def reference(alignment_input, alignment_mask, residue_mask, left_weight, right_weight, output_weight, pairwise_gradient):
    normalized_input, inverse_deviation = layer_normalize(alignment_input)
    presence_mask = alignment_mask.astype(jnp.float32)
    left = project(normalized_input, left_weight, presence_mask)
    right = project(normalized_input, right_weight, presence_mask)
    counts = jnp.dot(presence_mask.T, presence_mask, precision=lax.Precision.HIGHEST) + 0.001
    residue = residue_mask.astype(pairwise_gradient.dtype)
    left_wide = left.astype(jnp.float32)
    right_wide = right.astype(jnp.float32)

    def one_block(right_total, block):
        begin = (block * NI).astype(jnp.int32)
        grad_rows = lax.dynamic_slice_in_dim(pairwise_gradient, begin, NI, 0)
        res_rows = lax.dynamic_slice_in_dim(residue, begin, NI, 0)
        masked_grad = grad_rows * (res_rows[:, None] * residue[None, :])[:, :, None]
        tiles = tile_grad(masked_grad, lax.dynamic_slice_in_dim(counts, begin, NI, 0), output_weight).astype(jnp.float32)
        left_rows = lax.dynamic_slice_in_dim(left_wide, begin, NI, 1)
        left_part = jnp.einsum('ijce,sje->sic', tiles, right_wide)
        right_total = right_total + jnp.einsum('ijce,sic->sje', tiles, left_rows)
        return (right_total, left_part)
    blocks = jnp.arange(RESIDUE_COUNT // NI, dtype=jnp.int32)
    right_sum, left_parts = lax.scan(one_block, jnp.zeros((SEQUENCE_COUNT, RESIDUE_COUNT, HIDDEN_CHANNELS), jnp.float32), blocks)
    left_sum = jnp.transpose(left_parts, (1, 0, 2, 3)).reshape(SEQUENCE_COUNT, RESIDUE_COUNT, HIDDEN_CHANNELS)
    left_grad = presence_mask[:, :, None] * left_sum
    right_grad = presence_mask[:, :, None] * right_sum
    normed_grad = jnp.einsum('snc,mc->snm', left_grad, left_weight.astype(jnp.float32), precision=lax.Precision.HIGHEST)
    normed_grad = normed_grad + jnp.einsum('snc,mc->snm', right_grad, right_weight.astype(jnp.float32), precision=lax.Precision.HIGHEST)
    mean_grad = lax.optimization_barrier(jnp.mean(normed_grad, axis=-1, keepdims=True))
    mean_cross = lax.optimization_barrier(jnp.mean(normed_grad * normalized_input, axis=-1, keepdims=True))
    return inverse_deviation * (normed_grad - mean_grad - normalized_input * mean_cross)
```

```python
import functools

import jax
import jax.numpy as jnp
from jax import lax
from jax.experimental import pallas as pl
from jax.experimental.pallas import tpu as pltpu
from jax.sharding import PartitionSpec as P

F32 = jnp.float32
BF16 = jnp.bfloat16
NT = (((1,), (1,)), ((), ()))
PARAMS = pltpu.CompilerParams(vmem_limit_bytes=56 * 1024 * 1024)


def iota(shape, axis):
    return lax.broadcasted_iota(jnp.int32, shape, axis)


def own_presence(mask, me, rows):
    pick = iota((mask.shape[1], rows), 0) == me * rows + iota((mask.shape[1], rows), 1)
    return jnp.dot(mask.astype(F32).astype(BF16), pick.astype(F32).astype(BF16), preferred_element_type=F32)


def presence_row(own, sequence_major):
    depth, rows = own.shape
    count = depth * rows
    column = iota((rows, count), 1)
    residue = column % rows if sequence_major else column // depth
    spread = (residue == iota((rows, count), 0)).astype(F32).astype(BF16)
    wide = jnp.dot(own.astype(BF16), spread, preferred_element_type=F32)
    column = iota((depth, count), 1)
    sequence = column // rows if sequence_major else column % depth
    return jnp.sum(jnp.where(sequence == iota((depth, count), 0), wide, 0.0), axis=0, keepdims=True)


def project_kernel(rows, x_ref, mask_ref, lw_ref, rw_ref, left_ref, right_ref, normed, flat):
    count, channels = x_ref.shape
    depth = count // rows
    hidden = lw_ref.shape[1]
    me = lax.axis_index("row")
    value = x_ref[...].astype(F32)
    centered = value - jnp.mean(value, axis=-1, keepdims=True)
    recip = lax.rsqrt(jnp.mean(centered * centered, axis=-1, keepdims=True) + 1e-05)
    value = centered * recip
    normed[...] = value
    own = own_presence(mask_ref[...], me, rows)
    rwt = rw_ref[...].astype(F32).T.astype(BF16)
    right = lax.dot_general(rwt, value.astype(BF16), NT, preferred_element_type=F32)
    right = right * presence_row(own, True)
    for s in range(depth):
        flat[pl.ds(s, hidden, stride=depth), :] = right[:, s * rows : (s + 1) * rows]
    right_ref[...] = flat[...].T.astype(BF16)
    by_residue = jnp.concatenate(
        [normed[pl.ds(i, depth, stride=rows), :] for i in range(rows)], axis=0
    ).astype(BF16)
    lwt = lw_ref[...].astype(F32).T.astype(BF16)
    left = lax.dot_general(lwt, by_residue, NT, preferred_element_type=F32)
    left_ref[...] = (left * presence_row(own, False)).astype(BF16)


def partial_kernel(
    rows, size, g_ref, mask_ref, res_ref, left_ref, ow_ref,
    keep_ref, send_ref, scaled_ref, owp_ref,
    inverse, ow_wide, stack, spread,
):
    depth, width = mask_ref.shape
    hidden = left_ref.shape[0]
    pair = g_ref.shape[2]
    me = lax.axis_index("row")
    bits = size.bit_length() - 1
    fold = 256 // hidden
    groups = hidden // fold
    mask = mask_ref[...].astype(F32)
    own = own_presence(mask_ref[...], me, rows)
    residue = res_ref[...].astype(F32)
    residue_own = own_presence(jnp.broadcast_to(res_ref[...], (8, width)), me, rows)[:1]
    tall = jnp.concatenate([mask, jnp.broadcast_to(residue, (8, width))], axis=0).T
    counts = jnp.dot(tall[:, :depth].astype(BF16), own.astype(BF16), preferred_element_type=F32) + 0.001
    inverse[...] = tall[:, depth : depth + 1] * residue_own / counts

    def scale(p, _):
        relative = 0
        for t in range(bits):
            relative = relative + (((p >> (bits - 1 - t)) & 1) << t)
        begin = pl.multiple_of((me ^ relative) * rows, rows)
        factor = inverse[pl.ds(begin, rows), :]
        for i in range(rows):
            block = g_ref[i, pl.ds(begin, rows), :].astype(F32) * factor[:, i : i + 1]
            scaled_ref[pl.ds(pl.multiple_of(p * rows, rows), rows), i * pair : (i + 1) * pair] = block.astype(BF16)
        return 0

    lax.fori_loop(0, size, scale, 0)
    ow_wide[...] = ow_ref[...].astype(F32)
    for e in range(hidden):
        owp_ref[e * hidden : (e + 1) * hidden, :] = ow_wide[pl.ds(e, hidden, stride=hidden), :].astype(BF16)
    for g in range(groups):
        stack[g * pair : (g + 1) * pair, :] = owp_ref[g * 256 : (g + 1) * 256, :].T
    per = 128 // depth
    blocks = rows // per
    tile = jnp.concatenate([left_ref[:, g * 128 : (g + 1) * 128] for g in range(blocks)], axis=0)
    column = iota((128, per * 256), 1)
    repeat = (column % depth + depth * (column // 256)) == iota((128, per * 256), 0)
    wide = jnp.dot(tile, repeat.astype(F32).astype(BF16), preferred_element_type=F32)
    diagonal = iota((256, 256), 0) // hidden == iota((256, 256), 1) // depth
    for i in range(rows):
        g, q = divmod(i, per)
        own_left = wide[g * hidden : (g + 1) * hidden, q * 256 : (q + 1) * 256]
        block = jnp.where(diagonal, jnp.concatenate([own_left] * fold, axis=0), 0.0).astype(BF16)
        out = jnp.dot(stack[...], block, preferred_element_type=F32).astype(BF16)
        for g in range(groups):
            spread[i * pair : (i + 1) * pair, g * 256 : (g + 1) * 256] = out[g * pair : (g + 1) * pair, :]
    half = width // 2
    send_ref[...] = jnp.dot(scaled_ref[half:, :], spread[...], preferred_element_type=F32).astype(BF16)
    keep_ref[...] = jnp.dot(scaled_ref[:half, :], spread[...], preferred_element_type=F32)


def left_kernel(
    rows, *refs,
):
    (*pieces, scaled_ref, owp_ref, x_ref, mask_ref, lw_ref, grad_ref, normed_ref, recip_ref, presence_ref,
     panel, outer, total) = refs
    count, channels = x_ref.shape
    depth = count // rows
    pair = owp_ref.shape[1]
    hidden = lw_ref.shape[1]
    me = lax.axis_index("row")
    begin = 0
    for piece in pieces:
        panel[begin : begin + piece.shape[0], :] = piece[...]
        begin += piece.shape[0]
    turned = panel[...].T
    for q in range(rows // 2):
        out = jnp.dot(turned, scaled_ref[:, q * 2 * pair : (q + 1) * 2 * pair], preferred_element_type=F32).astype(BF16)
        for h in range(2):
            i = 2 * q + h
            outer[:, i * depth : (i + 1) * depth, :] = out[:, h * pair : (h + 1) * pair].reshape(hidden, depth, pair)
    acc = jnp.zeros((count, hidden), F32)
    for e in range(0, hidden, 2):
        lhs = jnp.concatenate([outer[e], outer[e + 1]], axis=1)
        rhs = jnp.concatenate([owp_ref[e * hidden : (e + 1) * hidden, :], owp_ref[(e + 1) * hidden : (e + 2) * hidden, :]], axis=1)
        acc = acc + lax.dot_general(lhs, rhs, NT, preferred_element_type=F32)
    total[...] = acc
    by_sequence = jnp.concatenate([total[pl.ds(s, rows, stride=depth), :] for s in range(depth)], axis=0)
    grad_ref[...] = lax.dot_general(
        lw_ref[...].astype(F32), by_sequence, NT, preferred_element_type=F32, precision=lax.Precision.HIGHEST
    )
    value = x_ref[...].astype(F32).T
    centered = value - jnp.mean(value, axis=0, keepdims=True)
    recip = lax.rsqrt(jnp.mean(centered * centered, axis=0, keepdims=True) + 1e-05)
    normed_ref[...] = centered * recip
    recip_ref[...] = recip
    presence_ref[...] = presence_row(own_presence(mask_ref[...], me, rows), True)


def final_kernel(rows, keep_ref, got_ref, rw_ref, grad_ref, normed_ref, recip_ref, presence_ref, out_ref, flat, lanes):
    hidden = rw_ref.shape[1]
    depth = keep_ref.shape[1] // hidden
    flat[...] = (keep_ref[...] + got_ref[...].astype(F32)).T
    for s in range(depth):
        lanes[:, s * rows : (s + 1) * rows] = flat[pl.ds(s, hidden, stride=depth), :]
    grad = jnp.dot(rw_ref[...].astype(F32), lanes[...], preferred_element_type=F32, precision=lax.Precision.HIGHEST)
    grad = (grad + grad_ref[...]) * presence_ref[...]
    normed = normed_ref[...]
    mean = jnp.mean(grad, axis=0, keepdims=True)
    cross = jnp.mean(grad * normed, axis=0, keepdims=True)
    out_ref[...] = (recip_ref[...] * (grad - mean - normed * cross)).T


def shape(dims, dtype):
    return jax.ShapeDtypeStruct(dims, dtype)


def shards(size, x, mask, residue_mask, lw, rw, ow, g):
    depth, rows, channels = x.shape
    hidden = lw.shape[1]
    width, pair = g.shape[1:]
    flat_width = depth * hidden
    x = x.reshape(depth * rows, channels)
    residue = residue_mask.reshape(1, width)
    vmem = pl.BlockSpec(memory_space=pltpu.VMEM)

    def exchange(value, bit):
        return lax.ppermute(value, "row", [(d, d ^ bit) for d in range(size)])

    left, right = pl.pallas_call(
        functools.partial(project_kernel, rows),
        out_shape=(shape((hidden, depth * rows), BF16), shape((rows, flat_width), BF16)),
        in_specs=[vmem] * 4,
        out_specs=(vmem, vmem),
        scratch_shapes=[pltpu.VMEM((depth * rows, channels), F32), pltpu.VMEM((flat_width, rows), F32)],
        compiler_params=PARAMS,
        name="project",
    )(x, mask, lw, rw)
    keep, send, scaled, owp = pl.pallas_call(
        functools.partial(partial_kernel, rows, size),
        out_shape=(
            shape((width // 2, flat_width), F32),
            shape((width // 2, flat_width), BF16),
            shape((width, rows * pair), BF16),
            shape(ow.shape, BF16),
        ),
        in_specs=[vmem] * 5,
        out_specs=(vmem,) * 4,
        scratch_shapes=[
            pltpu.VMEM((width, rows), F32),
            pltpu.VMEM(ow.shape, F32),
            pltpu.VMEM((ow.shape[0] // 256 * pair, 256), BF16),
            pltpu.VMEM((rows * pair, flat_width), BF16),
        ],
        compiler_params=PARAMS,
        cost_estimate=pl.CostEstimate(flops=4 * 2**30, bytes_accessed=4 << 20, transcendentals=0),
        name="partial",
    )(g, mask, residue, left, ow)
    pieces = [right]
    bit = size // 2
    while bit:
        block = pieces[0] if len(pieces) == 1 else jnp.concatenate(pieces, axis=0)
        pieces.append(exchange(block, bit))
        bit //= 2
    bit = 1
    got = exchange(send, bit)
    while keep.shape[0] > rows:
        total = keep + got.astype(F32)
        half = total.shape[0] // 2
        bit *= 2
        keep = total[:half]
        got = exchange(total[half:].astype(BF16), bit)
    grad, normed, recip, presence = pl.pallas_call(
        functools.partial(left_kernel, rows),
        out_shape=(
            shape((channels, depth * rows), F32),
            shape((channels, depth * rows), F32),
            shape((1, depth * rows), F32),
            shape((1, depth * rows), F32),
        ),
        in_specs=[vmem] * (len(pieces) + 5),
        out_specs=(vmem,) * 4,
        scratch_shapes=[
            pltpu.VMEM((width, flat_width), BF16),
            pltpu.VMEM((hidden, depth * rows, pair), BF16),
            pltpu.VMEM((depth * rows, hidden), F32),
        ],
        compiler_params=PARAMS,
        cost_estimate=pl.CostEstimate(flops=4 * 2**30, bytes_accessed=4 << 20, transcendentals=0),
        name="left",
    )(*pieces, scaled, owp, x, mask, lw)
    out = pl.pallas_call(
        functools.partial(final_kernel, rows),
        out_shape=shape((depth * rows, channels), F32),
        in_specs=[vmem] * 7,
        out_specs=vmem,
        scratch_shapes=[pltpu.VMEM((flat_width, rows), F32), pltpu.VMEM((hidden, depth * rows), F32)],
        compiler_params=PARAMS,
        name="final",
    )(keep, got, rw, grad, normed, recip, presence)
    return out.reshape(depth, rows, channels)


def solution(mesh):
    return jax.shard_map(
        functools.partial(shards, mesh.shape["row"]),
        mesh=mesh,
        in_specs=(
            P("groups", "row", None),
            P("groups", None),
            P("groups"),
            P(),
            P(),
            P(),
            P(("groups", "row"), None, None),
        ),
        out_specs=P("groups", "row", None),
        check_vma=False,
    )
```

```python
import functools

import jax
import jax.numpy as jnp
from jax import lax
from jax.experimental import pallas as pl
from jax.experimental.pallas import tpu as pltpu
from jax.sharding import PartitionSpec as P

F32 = jnp.float32
BF16 = jnp.bfloat16
NT = (((1,), (1,)), ((), ()))
PARAMS = pltpu.CompilerParams(vmem_limit_bytes=24 * 1024 * 1024)


def iota(shape, axis):
    return lax.broadcasted_iota(jnp.int32, shape, axis)


def own_presence(mask, me, rows):
    pick = iota((mask.shape[1], rows), 0) == me * rows + iota((mask.shape[1], rows), 1)
    return jnp.dot(mask.astype(F32).astype(BF16), pick.astype(F32).astype(BF16), preferred_element_type=F32)


def presence_row(own, sequence_major):
    depth, rows = own.shape
    count = depth * rows
    column = iota((rows, count), 1)
    residue = column % rows if sequence_major else column // depth
    spread = (residue == iota((rows, count), 0)).astype(F32).astype(BF16)
    wide = jnp.dot(own.astype(BF16), spread, preferred_element_type=F32)
    column = iota((depth, count), 1)
    sequence = column // rows if sequence_major else column % depth
    return jnp.sum(jnp.where(sequence == iota((depth, count), 0), wide, 0.0), axis=0, keepdims=True)


def project_kernel(
    rows,
    x_far, mask_far, res_far, lw_far, rw_far, ow_far, g_far,
    left_ref, right_ref, x_ref, mask_ref, lw_ref, rw_ref, owp_ref, stack_ref, inverse_ref, g_ref,
    res_ref, ow_ref, normed, flat, ow_wide, arrived,
):
    sources = (x_far, mask_far, res_far, lw_far, rw_far, ow_far, g_far)
    targets = (x_ref, mask_ref, res_ref, lw_ref, rw_ref, ow_ref, g_ref)
    copies = [pltpu.make_async_copy(a, b, arrived.at[t]) for t, (a, b) in enumerate(zip(sources, targets))]
    for copy in copies:
        copy.start()
    for copy in copies[:-1]:
        copy.wait()
    count, channels = x_ref.shape
    depth, width = mask_ref.shape
    hidden = lw_ref.shape[0]
    pair = ow_ref.shape[1]
    me = lax.axis_index("row")
    value = x_ref[...].astype(F32)
    centered = value - jnp.mean(value, axis=-1, keepdims=True)
    recip = lax.rsqrt(jnp.mean(centered * centered, axis=-1, keepdims=True) + 1e-05)
    value = centered * recip
    normed[...] = value
    own = own_presence(mask_ref[...], me, rows)
    right = lax.dot_general(rw_ref[...], value.astype(BF16), NT, preferred_element_type=F32)
    right = right * presence_row(own, True)
    for s in range(depth):
        flat[pl.ds(s, hidden, stride=depth), :] = right[:, s * rows : (s + 1) * rows]
    right_ref[...] = flat[...].T.astype(BF16)
    by_residue = jnp.concatenate(
        [normed[pl.ds(i, depth, stride=rows), :] for i in range(rows)], axis=0
    ).astype(BF16)
    left = lax.dot_general(lw_ref[...], by_residue, NT, preferred_element_type=F32)
    left_ref[...] = (left * presence_row(own, False)).astype(BF16)
    mask = mask_ref[...].astype(F32)
    residue = res_ref[...].astype(F32)
    residue_own = own_presence(jnp.broadcast_to(res_ref[...], (8, width)), me, rows)[:1]
    tall = jnp.concatenate([mask, jnp.broadcast_to(residue, (8, width))], axis=0).T
    counts = jnp.dot(tall[:, :depth].astype(BF16), own.astype(BF16), preferred_element_type=F32) + 0.001
    inverse_ref[...] = tall[:, depth : depth + 1] * residue_own / counts
    ow_wide[...] = ow_ref[...].astype(F32)
    for e in range(hidden):
        owp_ref[e * hidden : (e + 1) * hidden, :] = ow_wide[pl.ds(e, hidden, stride=hidden), :].astype(BF16)
    for g in range(hidden * hidden // 256):
        stack_ref[g * pair : (g + 1) * pair, :] = owp_ref[g * 256 : (g + 1) * 256, :].T
    copies[-1].wait()


def spread_kernel(rows, size, g_ref, inverse_ref, left_ref, stack_ref, scaled_ref, spread_ref):
    hidden, count = left_ref.shape
    depth = count // rows
    pair = g_ref.shape[2]
    me = lax.axis_index("row")
    bits = size.bit_length() - 1
    fold = 256 // hidden
    groups = hidden // fold
    per = 128 // depth
    blocks = rows // per
    tile = jnp.concatenate([left_ref[:, g * 128 : (g + 1) * 128] for g in range(blocks)], axis=0)
    column = iota((128, per * 256), 1)
    repeat = (column % depth + depth * (column // 256)) == iota((128, per * 256), 0)
    wide = jnp.dot(tile, repeat.astype(F32).astype(BF16), preferred_element_type=F32)
    diagonal = iota((256, 256), 0) // hidden == iota((256, 256), 1) // depth
    for i in range(rows):
        g, q = divmod(i, per)
        own_left = wide[g * hidden : (g + 1) * hidden, q * 256 : (q + 1) * 256]
        block = jnp.where(diagonal, jnp.concatenate([own_left] * fold, axis=0), 0.0).astype(BF16)
        out = jnp.dot(stack_ref[...], block, preferred_element_type=F32).astype(BF16)
        for g in range(groups):
            spread_ref[i * pair : (i + 1) * pair, g * 256 : (g + 1) * 256] = out[g * pair : (g + 1) * pair, :]
        for p in range(i * size // rows, (i + 1) * size // rows):
            relative = sum(((p >> (bits - 1 - t)) & 1) << t for t in range(bits))
            begin = pl.multiple_of((me ^ relative) * rows, rows)
            factor = inverse_ref[pl.ds(begin, rows), :]
            for h in range(rows):
                part = g_ref[h, pl.ds(begin, rows), :].astype(F32) * factor[:, h : h + 1]
                scaled_ref[p * rows : (p + 1) * rows, h * pair : (h + 1) * pair] = part.astype(BF16)


def send_kernel(scaled_ref, spread_ref, send_ref):
    half = send_ref.shape[0]
    send_ref[...] = jnp.dot(scaled_ref[half:, :], spread_ref[...], preferred_element_type=F32).astype(BF16)


def keep_kernel(rows, scaled_ref, spread_ref, x_ref, mask_ref, keep_ref, normed_ref, recip_ref, presence_ref):
    half = keep_ref.shape[0]
    keep_ref[...] = jnp.dot(scaled_ref[:half, :], spread_ref[...], preferred_element_type=F32)
    value = x_ref[...].astype(F32).T
    centered = value - jnp.mean(value, axis=0, keepdims=True)
    recip = lax.rsqrt(jnp.mean(centered * centered, axis=0, keepdims=True) + 1e-05)
    normed_ref[...] = centered * recip
    recip_ref[...] = recip
    presence_ref[...] = presence_row(own_presence(mask_ref[...], lax.axis_index("row"), rows), True)


def left_kernel(rows, near_ref, far_ref, scaled_ref, owp_ref, lw_ref, grad_ref, turned, outer, total):
    hidden = lw_ref.shape[0]
    count = total.shape[0]
    depth = count // rows
    pair = owp_ref.shape[1]
    half = near_ref.shape[0]
    turned[:, :half] = near_ref[...].T
    turned[:, half:] = far_ref[...].T
    for q in range(rows // 2):
        out = jnp.dot(
            turned[...], scaled_ref[:, q * 2 * pair : (q + 1) * 2 * pair], preferred_element_type=F32
        ).astype(BF16)
        for h in range(2):
            i = 2 * q + h
            outer[:, i * depth : (i + 1) * depth, :] = out[:, h * pair : (h + 1) * pair].reshape(hidden, depth, pair)
    acc = jnp.zeros((count, hidden), F32)
    for e in range(0, hidden, 2):
        lhs = jnp.concatenate([outer[e], outer[e + 1]], axis=1)
        rhs = jnp.concatenate(
            [owp_ref[e * hidden : (e + 1) * hidden, :], owp_ref[(e + 1) * hidden : (e + 2) * hidden, :]], axis=1
        )
        acc = acc + lax.dot_general(lhs, rhs, NT, preferred_element_type=F32)
    total[...] = acc
    by_sequence = jnp.concatenate([total[pl.ds(s, rows, stride=depth), :] for s in range(depth)], axis=0)
    grad_ref[...] = lax.dot_general(
        lw_ref[...].astype(F32).T, by_sequence, NT, preferred_element_type=F32, precision=lax.Precision.HIGHEST
    )


def final_kernel(rows, keep_ref, got_ref, rw_ref, grad_ref, normed_ref, recip_ref, presence_ref, out_ref, flat, lanes):
    hidden = rw_ref.shape[0]
    depth = keep_ref.shape[1] // hidden
    flat[...] = (keep_ref[...] + got_ref[...].astype(F32)).T
    for s in range(depth):
        lanes[:, s * rows : (s + 1) * rows] = flat[pl.ds(s, hidden, stride=depth), :]
    grad = jnp.dot(
        rw_ref[...].astype(F32).T, lanes[...], preferred_element_type=F32, precision=lax.Precision.HIGHEST
    )
    grad = (grad + grad_ref[...]) * presence_ref[...]
    normed = normed_ref[...]
    mean = jnp.mean(grad, axis=0, keepdims=True)
    cross = jnp.mean(grad * normed, axis=0, keepdims=True)
    out_ref[...] = (recip_ref[...] * (grad - mean - normed * cross)).T


def near_shape(dims, dtype):
    return pltpu.VMEM(dims, dtype)


def near(value):
    return pltpu.with_memory_space_constraint(value, pltpu.VMEM)


def far(value):
    return pltpu.with_memory_space_constraint(value, pltpu.HBM)


def call(kernel, name, out_shape, args, scratch=(), flops=0, in_specs=None):
    vmem = pl.BlockSpec(memory_space=pltpu.VMEM)
    out_specs = (vmem,) * len(out_shape) if isinstance(out_shape, tuple) else vmem
    return pl.pallas_call(
        kernel,
        out_shape=out_shape,
        in_specs=in_specs or [vmem] * len(args),
        out_specs=out_specs,
        scratch_shapes=scratch,
        compiler_params=PARAMS,
        cost_estimate=pl.CostEstimate(flops=flops, bytes_accessed=1 << 20, transcendentals=0),
        name=name,
    )(*args)


def shards(size, x, mask, residue_mask, lw, rw, ow, g):
    depth, rows, channels = x.shape
    hidden = lw.shape[1]
    width, pair = g.shape[1:]
    count = depth * rows
    flat_width = depth * hidden

    def exchange(value, bit):
        return lax.ppermute(value, "row", [(d, d ^ bit) for d in range(size)])

    sources = (x.reshape(count, channels), mask, residue_mask.reshape(1, width), lw.T, rw.T, ow, g)
    left, right, x, mask, lw, rw, owp, stack, inverse, g = call(
        functools.partial(project_kernel, rows),
        "project",
        (
            near_shape((hidden, count), BF16),
            near_shape((rows, flat_width), BF16),
            near_shape((count, channels), BF16),
            near_shape(mask.shape, mask.dtype),
            near_shape((hidden, channels), BF16),
            near_shape((hidden, channels), BF16),
            near_shape(ow.shape, BF16),
            near_shape((ow.shape[0] // 256 * pair, 256), BF16),
            near_shape((width, rows), F32),
            near_shape(g.shape, BF16),
        ),
        [far(v) for v in sources],
        [
            pltpu.VMEM((1, width), residue_mask.dtype),
            pltpu.VMEM(ow.shape, BF16),
            pltpu.VMEM((count, channels), F32),
            pltpu.VMEM((flat_width, rows), F32),
            pltpu.VMEM(ow.shape, F32),
            pltpu.SemaphoreType.DMA((len(sources),)),
        ],
        in_specs=[pl.BlockSpec(memory_space=pl.ANY)] * len(sources),
    )
    block = right
    bits = [1 << t for t in range(size.bit_length() - 1)]
    gathers = bits[::-1]

    def gather(block):
        return exchange(block, gathers.pop(0))

    early = gather(block)
    scaled, spread = call(
        functools.partial(spread_kernel, rows, size),
        "spread",
        (near_shape((width, rows * pair), BF16), near_shape((rows * pair, flat_width), BF16)),
        [near(v) for v in (g, inverse, left, stack)],
        flops=2 * 2**30,
    )
    early, spread = lax.optimization_barrier((early, spread))
    block = jnp.concatenate([block, early], axis=0)
    early = gather(block)
    send = call(
        send_kernel,
        "send",
        near_shape((width // 2, flat_width), BF16),
        [near(scaled), near(spread)],
        flops=2**30,
    )
    got = exchange(send, bits[0])
    keep, normed, recip, presence = call(
        functools.partial(keep_kernel, rows),
        "keep",
        (
            near_shape((width // 2, flat_width), F32),
            near_shape((channels, count), F32),
            near_shape((1, count), F32),
            near_shape((1, count), F32),
        ),
        [near(v) for v in (scaled, spread, x, mask)],
        flops=2**30,
    )
    for bit in bits[1:]:
        total = keep + got.astype(F32)
        half = total.shape[0] // 2
        keep = total[:half]
        got = exchange(total[half:].astype(BF16), bit)
        if block.shape[0] < width // 2:
            block = jnp.concatenate([block, early], axis=0)
            early = gather(block)
    while block.shape[0] < width // 2:
        block = jnp.concatenate([block, early], axis=0)
        early = gather(block)
    grad = call(
        functools.partial(left_kernel, rows),
        "left",
        near_shape((channels, count), F32),
        [near(v) for v in (block, early, scaled, owp, lw)],
        [
            pltpu.VMEM((flat_width, width), BF16),
            pltpu.VMEM((hidden, count, pair), BF16),
            pltpu.VMEM((count, hidden), F32),
        ],
        flops=4 * 2**30,
    )
    out = call(
        functools.partial(final_kernel, rows),
        "final",
        jax.ShapeDtypeStruct((count, channels), F32),
        [near(v) for v in (keep, got, rw, grad, normed, recip, presence)],
        [pltpu.VMEM((flat_width, rows), F32), pltpu.VMEM((hidden, count), F32)],
    )
    return out.reshape(depth, rows, channels)


def solution(mesh):
    return jax.shard_map(
        functools.partial(shards, mesh.shape["row"]),
        mesh=mesh,
        in_specs=(
            P("groups", "row", None),
            P("groups", None),
            P("groups"),
            P(),
            P(),
            P(),
            P(("groups", "row"), None, None),
        ),
        out_specs=P("groups", "row", None),
        check_vma=False,
    )
```

```python
import functools

import jax
import jax.numpy as jnp
from jax import lax
from jax.experimental import pallas as pl
from jax.experimental.pallas import tpu as pltpu
from jax.sharding import PartitionSpec as P

F32 = jnp.float32
BF16 = jnp.bfloat16
NT = (((1,), (1,)), ((), ()))
PARAMS = pltpu.CompilerParams(vmem_limit_bytes=24 * 1024 * 1024)


def iota(shape, axis):
    return lax.broadcasted_iota(jnp.int32, shape, axis)


def own_presence(mask, me, rows):
    pick = iota((mask.shape[1], rows), 0) == me * rows + iota((mask.shape[1], rows), 1)
    return jnp.dot(mask.astype(F32).astype(BF16), pick.astype(F32).astype(BF16), preferred_element_type=F32)


def presence_row(own, sequence_major):
    depth, rows = own.shape
    count = depth * rows
    column = iota((rows, count), 1)
    residue = column % rows if sequence_major else column // depth
    spread = (residue == iota((rows, count), 0)).astype(F32).astype(BF16)
    wide = jnp.dot(own.astype(BF16), spread, preferred_element_type=F32)
    column = iota((depth, count), 1)
    sequence = column // rows if sequence_major else column % depth
    return jnp.sum(jnp.where(sequence == iota((depth, count), 0), wide, 0.0), axis=0, keepdims=True)


def project_kernel(
    rows,
    x_far, mask_far, res_far, lw_far, rw_far, ow_far, g_far,
    left_ref, right_ref, x_ref, mask_ref, lw_ref, rw_ref, owp_ref, stack_ref, inverse_ref, g_ref,
    res_ref, ow_ref, normed, flat, ow_wide, arrived,
):
    sources = (x_far, mask_far, res_far, lw_far, rw_far, ow_far, g_far)
    targets = (x_ref, mask_ref, res_ref, lw_ref, rw_ref, ow_ref, g_ref)
    copies = [pltpu.make_async_copy(a, b, arrived.at[t]) for t, (a, b) in enumerate(zip(sources, targets))]
    for copy in copies:
        copy.start()
    for copy in copies[:-1]:
        copy.wait()
    count, channels = x_ref.shape
    depth, width = mask_ref.shape
    hidden = lw_ref.shape[0]
    pair = ow_ref.shape[1]
    me = lax.axis_index("row")
    value = x_ref[...].astype(F32)
    centered = value - jnp.mean(value, axis=-1, keepdims=True)
    recip = lax.rsqrt(jnp.mean(centered * centered, axis=-1, keepdims=True) + 1e-05)
    value = centered * recip
    normed[...] = value
    own = own_presence(mask_ref[...], me, rows)
    right = lax.dot_general(rw_ref[...], value.astype(BF16), NT, preferred_element_type=F32)
    right = right * presence_row(own, True)
    for s in range(depth):
        flat[pl.ds(s, hidden, stride=depth), :] = right[:, s * rows : (s + 1) * rows]
    right_ref[...] = flat[...].T.astype(BF16)
    by_residue = jnp.concatenate(
        [normed[pl.ds(i, depth, stride=rows), :] for i in range(rows)], axis=0
    ).astype(BF16)
    left = lax.dot_general(lw_ref[...], by_residue, NT, preferred_element_type=F32)
    left_ref[...] = (left * presence_row(own, False)).astype(BF16)
    mask = mask_ref[...].astype(F32)
    residue = res_ref[...].astype(F32)
    residue_own = own_presence(jnp.broadcast_to(res_ref[...], (8, width)), me, rows)[:1]
    tall = jnp.concatenate([mask, jnp.broadcast_to(residue, (8, width))], axis=0).T
    counts = jnp.dot(tall[:, :depth].astype(BF16), own.astype(BF16), preferred_element_type=F32) + 0.001
    inverse_ref[...] = tall[:, depth : depth + 1] * residue_own / counts
    ow_wide[...] = ow_ref[...].astype(F32)
    for e in range(hidden):
        owp_ref[e * hidden : (e + 1) * hidden, :] = ow_wide[pl.ds(e, hidden, stride=hidden), :].astype(BF16)
    for g in range(hidden * hidden // 256):
        stack_ref[g * pair : (g + 1) * pair, :] = owp_ref[g * 256 : (g + 1) * 256, :].T
    copies[-1].wait()


def spread_kernel(rows, size, g_ref, inverse_ref, left_ref, stack_ref, scaled_ref, spread_ref):
    hidden, count = left_ref.shape
    depth = count // rows
    pair = g_ref.shape[2]
    me = lax.axis_index("row")
    bits = size.bit_length() - 1
    fold = 256 // hidden
    groups = hidden // fold
    per = 128 // depth
    blocks = rows // per
    tile = jnp.concatenate([left_ref[:, g * 128 : (g + 1) * 128] for g in range(blocks)], axis=0)
    column = iota((128, per * 256), 1)
    repeat = (column % depth + depth * (column // 256)) == iota((128, per * 256), 0)
    wide = jnp.dot(tile, repeat.astype(F32).astype(BF16), preferred_element_type=F32)
    diagonal = iota((256, 256), 0) // hidden == iota((256, 256), 1) // depth
    for i in range(rows):
        g, q = divmod(i, per)
        own_left = wide[g * hidden : (g + 1) * hidden, q * 256 : (q + 1) * 256]
        block = jnp.where(diagonal, jnp.concatenate([own_left] * fold, axis=0), 0.0).astype(BF16)
        out = jnp.dot(stack_ref[...], block, preferred_element_type=F32).astype(BF16)
        for g in range(groups):
            spread_ref[i * pair : (i + 1) * pair, g * 256 : (g + 1) * 256] = out[g * pair : (g + 1) * pair, :]
        for p in range(i * size // rows, (i + 1) * size // rows):
            relative = sum(((p >> (bits - 1 - t)) & 1) << t for t in range(bits))
            begin = pl.multiple_of((me ^ relative) * rows, rows)
            factor = inverse_ref[pl.ds(begin, rows), :]
            for h in range(rows):
                part = g_ref[h, pl.ds(begin, rows), :].astype(F32) * factor[:, h : h + 1]
                scaled_ref[p * rows : (p + 1) * rows, h * pair : (h + 1) * pair] = part.astype(BF16)


def send_kernel(scaled_ref, spread_ref, send_ref):
    half = send_ref.shape[0]
    send_ref[...] = jnp.dot(scaled_ref[half:, :], spread_ref[...], preferred_element_type=F32).astype(BF16)


def keep_kernel(rows, scaled_ref, spread_ref, x_ref, mask_ref, keep_ref, normed_ref, recip_ref, presence_ref):
    half = keep_ref.shape[0]
    keep_ref[...] = jnp.dot(scaled_ref[:half, :], spread_ref[...], preferred_element_type=F32)
    value = x_ref[...].astype(F32).T
    centered = value - jnp.mean(value, axis=0, keepdims=True)
    recip = lax.rsqrt(jnp.mean(centered * centered, axis=0, keepdims=True) + 1e-05)
    normed_ref[...] = centered * recip
    recip_ref[...] = recip
    presence_ref[...] = presence_row(own_presence(mask_ref[...], lax.axis_index("row"), rows), True)


def weigh(weight, value):
    high = value.astype(BF16)
    low = (value - high.astype(F32)).astype(BF16)
    turned = weight.astype(F32).T.astype(BF16)
    return jnp.dot(
        jnp.concatenate([turned, turned], axis=1), jnp.concatenate([high, low], axis=0), preferred_element_type=F32
    )


def outer_kernel(rows, near_ref, far_ref, scaled_ref, outer_ref, turned):
    hidden, count, pair = outer_ref.shape
    depth = count // rows
    half = near_ref.shape[0]
    turned[:, :half] = near_ref[...].T
    turned[:, half:] = far_ref[...].T
    for q in range(rows // 2):
        out = jnp.dot(
            turned[...], scaled_ref[:, q * 2 * pair : (q + 1) * 2 * pair], preferred_element_type=F32
        ).astype(BF16)
        for h in range(2):
            i = 2 * q + h
            outer_ref[:, i * depth : (i + 1) * depth, :] = out[:, h * pair : (h + 1) * pair].reshape(hidden, depth, pair)


def left_kernel(rows, outer_ref, owp_ref, lw_ref, grad_ref, total):
    hidden = lw_ref.shape[0]
    count = total.shape[0]
    depth = count // rows
    acc = jnp.zeros((count, hidden), F32)
    for e in range(0, hidden, 2):
        lhs = jnp.concatenate([outer_ref[e], outer_ref[e + 1]], axis=1)
        rhs = jnp.concatenate(
            [owp_ref[e * hidden : (e + 1) * hidden, :], owp_ref[(e + 1) * hidden : (e + 2) * hidden, :]], axis=1
        )
        acc = acc + lax.dot_general(lhs, rhs, NT, preferred_element_type=F32)
    total[...] = acc
    by_sequence = jnp.concatenate([total[pl.ds(s, rows, stride=depth), :] for s in range(depth)], axis=0)
    grad_ref[...] = weigh(lw_ref[...], by_sequence.T)


def final_kernel(rows, keep_ref, *refs):
    *got_refs, rw_ref, grad_ref, normed_ref, recip_ref, presence_ref, out_ref, flat, lanes = refs
    hidden = rw_ref.shape[0]
    depth = keep_ref.shape[1] // hidden
    total = keep_ref[...]
    for got_ref in got_refs:
        total = total + got_ref[...].astype(F32)
    flat[...] = total.T
    for s in range(depth):
        lanes[:, s * rows : (s + 1) * rows] = flat[pl.ds(s, hidden, stride=depth), :]
    grad = (weigh(rw_ref[...], lanes[...]) + grad_ref[...]) * presence_ref[...]
    normed = normed_ref[...]
    mean = jnp.mean(grad, axis=0, keepdims=True)
    cross = jnp.mean(grad * normed, axis=0, keepdims=True)
    out_ref[...] = (recip_ref[...] * (grad - mean - normed * cross)).T


def near_shape(dims, dtype):
    return pltpu.VMEM(dims, dtype)


def near(value):
    return pltpu.with_memory_space_constraint(value, pltpu.VMEM)


def far(value):
    return pltpu.with_memory_space_constraint(value, pltpu.HBM)


def call(kernel, name, out_shape, args, scratch=(), flops=0, in_specs=None):
    vmem = pl.BlockSpec(memory_space=pltpu.VMEM)
    out_specs = (vmem,) * len(out_shape) if isinstance(out_shape, tuple) else vmem
    return pl.pallas_call(
        kernel,
        out_shape=out_shape,
        in_specs=in_specs or [vmem] * len(args),
        out_specs=out_specs,
        scratch_shapes=scratch,
        compiler_params=PARAMS,
        cost_estimate=pl.CostEstimate(flops=flops, bytes_accessed=1 << 20, transcendentals=0),
        name=name,
    )(*args)


def shards(size, x, mask, residue_mask, lw, rw, ow, g):
    depth, rows, channels = x.shape
    hidden = lw.shape[1]
    width, pair = g.shape[1:]
    count = depth * rows
    flat_width = depth * hidden

    def exchange(value, bit):
        return lax.ppermute(value, "row", [(d, d ^ bit) for d in range(size)])

    sources = (x.reshape(count, channels), mask, residue_mask.reshape(1, width), lw.T, rw.T, ow, g)
    left, right, x, mask, lw, rw, owp, stack, inverse, g = call(
        functools.partial(project_kernel, rows),
        "project",
        (
            near_shape((hidden, count), BF16),
            near_shape((rows, flat_width), BF16),
            near_shape((count, channels), BF16),
            near_shape(mask.shape, mask.dtype),
            near_shape((hidden, channels), BF16),
            near_shape((hidden, channels), BF16),
            near_shape(ow.shape, BF16),
            near_shape((ow.shape[0] // 256 * pair, 256), BF16),
            near_shape((width, rows), F32),
            near_shape(g.shape, BF16),
        ),
        [far(v) for v in sources],
        [
            pltpu.VMEM((1, width), residue_mask.dtype),
            pltpu.VMEM(ow.shape, BF16),
            pltpu.VMEM((count, channels), F32),
            pltpu.VMEM((flat_width, rows), F32),
            pltpu.VMEM(ow.shape, F32),
            pltpu.SemaphoreType.DMA((len(sources),)),
        ],
        in_specs=[pl.BlockSpec(memory_space=pl.ANY)] * len(sources),
    )
    bits = [1 << t for t in range(size.bit_length() - 1)]
    stages = [bits[:1]] + [bits[t : t + 2] for t in range(1, len(bits), 2)]

    def partners(stage):
        found = [0]
        for bit in reversed(stage):
            found = found + [bit ^ f for f in found]
        return found

    def gather(blocks, stage):
        block = jnp.concatenate(blocks, axis=0) if len(blocks) > 1 else blocks[0]
        return [block] + [exchange(block, other) for other in partners(stage)[:0:-1]][::-1]

    def scatter(total, stage):
        others = partners(stage)
        part = total.shape[0] // len(others)
        got = [
            exchange(total[t * part : (t + 1) * part].astype(BF16), others[t]) for t in range(len(others) - 1, 0, -1)
        ]
        return total[:part], got

    blocks = gather([right], stages[-1])
    scaled, spread = call(
        functools.partial(spread_kernel, rows, size),
        "spread",
        (near_shape((width, rows * pair), BF16), near_shape((rows * pair, flat_width), BF16)),
        [near(v) for v in (g, inverse, left, stack)],
        flops=2 * 2**30,
    )
    blocks, spread = lax.optimization_barrier((blocks, spread))
    send = call(
        send_kernel,
        "send",
        near_shape((width // 2, flat_width), BF16),
        [near(scaled), near(spread)],
        flops=2**30,
    )
    got = exchange(send, bits[0])
    keep, normed, recip, presence = call(
        functools.partial(keep_kernel, rows),
        "keep",
        (
            near_shape((width // 2, flat_width), F32),
            near_shape((channels, count), F32),
            near_shape((1, count), F32),
            near_shape((1, count), F32),
        ),
        [near(v) for v in (scaled, spread, x, mask)],
        flops=2**30,
    )
    got = [got]
    for number, stage in enumerate(stages[1:], 1):
        for piece in got:
            keep = keep + piece.astype(F32)
        keep, got = scatter(keep, stage)
        if number < len(stages) - 1:
            blocks, keep = lax.optimization_barrier((blocks, keep))
            blocks = gather(blocks, stages[-1 - number])
    near_block, far_block = gather(blocks, stages[0])
    outer = call(
        functools.partial(outer_kernel, rows),
        "outer",
        near_shape((hidden, count, pair), BF16),
        [near(v) for v in (near_block, far_block, scaled)],
        [pltpu.VMEM((flat_width, width), BF16)],
        flops=2**26,
    )
    grad = call(
        functools.partial(left_kernel, rows),
        "left",
        near_shape((channels, count), F32),
        [near(v) for v in (outer, owp, lw)],
        [pltpu.VMEM((count, hidden), F32)],
        flops=2**26,
    )
    out = call(
        functools.partial(final_kernel, rows),
        "final",
        jax.ShapeDtypeStruct((count, channels), F32),
        [near(v) for v in (keep, *got, rw, grad, normed, recip, presence)],
        [pltpu.VMEM((flat_width, rows), F32), pltpu.VMEM((hidden, count), F32)],
    )
    return out.reshape(depth, rows, channels)


def solution(mesh):
    return jax.shard_map(
        functools.partial(shards, mesh.shape["row"]),
        mesh=mesh,
        in_specs=(
            P("groups", "row", None),
            P("groups", None),
            P("groups"),
            P(),
            P(),
            P(),
            P(("groups", "row"), None, None),
        ),
        out_specs=P("groups", "row", None),
        check_vma=False,
    )
```

```python
import functools

import jax
import jax.numpy as jnp
from jax import lax
from jax.experimental import pallas as pl
from jax.experimental.pallas import tpu as pltpu
from jax.sharding import PartitionSpec as P

F32 = jnp.float32
BF16 = jnp.bfloat16
NT = (((1,), (1,)), ((), ()))
PARAMS = pltpu.CompilerParams(vmem_limit_bytes=24 * 1024 * 1024)


def iota(shape, axis):
    return lax.broadcasted_iota(jnp.int32, shape, axis)


def own_presence(mask, me, rows):
    pick = iota((mask.shape[1], rows), 0) == me * rows + iota((mask.shape[1], rows), 1)
    return jnp.dot(mask.astype(F32).astype(BF16), pick.astype(F32).astype(BF16), preferred_element_type=F32)


def presence_row(own, sequence_major):
    depth, rows = own.shape
    count = depth * rows
    column = iota((rows, count), 1)
    residue = column % rows if sequence_major else column // depth
    spread = (residue == iota((rows, count), 0)).astype(F32).astype(BF16)
    wide = jnp.dot(own.astype(BF16), spread, preferred_element_type=F32)
    column = iota((depth, count), 1)
    sequence = column // rows if sequence_major else column % depth
    return jnp.sum(jnp.where(sequence == iota((depth, count), 0), wide, 0.0), axis=0, keepdims=True)


def project_kernel(
    rows,
    x_far, mask_far, res_far, lw_far, rw_far, ow_far, g_far,
    left_ref, right_ref, x_ref, mask_ref, lw_ref, rw_ref, owp_ref, stack_ref, inverse_ref, g_ref,
    res_ref, ow_ref, normed, flat, ow_wide, arrived,
):
    sources = (x_far, mask_far, res_far, lw_far, rw_far, ow_far, g_far)
    targets = (x_ref, mask_ref, res_ref, lw_ref, rw_ref, ow_ref, g_ref)
    copies = [pltpu.make_async_copy(a, b, arrived.at[t]) for t, (a, b) in enumerate(zip(sources, targets))]
    for copy in copies:
        copy.start()
    for copy in copies[:-1]:
        copy.wait()
    count, channels = x_ref.shape
    depth, width = mask_ref.shape
    hidden = lw_ref.shape[0]
    pair = ow_ref.shape[1]
    me = lax.axis_index("row")
    value = x_ref[...].astype(F32)
    centered = value - jnp.mean(value, axis=-1, keepdims=True)
    recip = lax.rsqrt(jnp.mean(centered * centered, axis=-1, keepdims=True) + 1e-05)
    value = centered * recip
    normed[...] = value
    own = own_presence(mask_ref[...], me, rows)
    right = lax.dot_general(rw_ref[...], value.astype(BF16), NT, preferred_element_type=F32)
    right = right * presence_row(own, True)
    for s in range(depth):
        flat[pl.ds(s, hidden, stride=depth), :] = right[:, s * rows : (s + 1) * rows]
    right_ref[...] = flat[...].T.astype(BF16)
    by_residue = jnp.concatenate(
        [normed[pl.ds(i, depth, stride=rows), :] for i in range(rows)], axis=0
    ).astype(BF16)
    left = lax.dot_general(lw_ref[...], by_residue, NT, preferred_element_type=F32)
    left_ref[...] = (left * presence_row(own, False)).astype(BF16)
    mask = mask_ref[...].astype(F32)
    residue = res_ref[...].astype(F32)
    residue_own = own_presence(jnp.broadcast_to(res_ref[...], (8, width)), me, rows)[:1]
    tall = jnp.concatenate([mask, jnp.broadcast_to(residue, (8, width))], axis=0).T
    counts = jnp.dot(tall[:, :depth].astype(BF16), own.astype(BF16), preferred_element_type=F32) + 0.001
    inverse_ref[...] = tall[:, depth : depth + 1] * residue_own / counts
    ow_wide[...] = ow_ref[...].astype(F32)
    for e in range(hidden):
        owp_ref[e * hidden : (e + 1) * hidden, :] = ow_wide[pl.ds(e, hidden, stride=hidden), :].astype(BF16)
    for g in range(hidden * hidden // 256):
        stack_ref[g * pair : (g + 1) * pair, :] = owp_ref[g * 256 : (g + 1) * 256, :].T
    copies[-1].wait()


def spread_kernel(rows, size, g_ref, inverse_ref, left_ref, stack_ref, scaled_ref, spread_ref):
    hidden, count = left_ref.shape
    depth = count // rows
    pair = g_ref.shape[2]
    me = lax.axis_index("row")
    bits = size.bit_length() - 1
    fold = 256 // hidden
    groups = hidden // fold
    per = 128 // depth
    blocks = rows // per
    tile = jnp.concatenate([left_ref[:, g * 128 : (g + 1) * 128] for g in range(blocks)], axis=0)
    column = iota((128, per * 256), 1)
    repeat = (column % depth + depth * (column // 256)) == iota((128, per * 256), 0)
    wide = jnp.dot(tile, repeat.astype(F32).astype(BF16), preferred_element_type=F32)
    diagonal = iota((256, 256), 0) // hidden == iota((256, 256), 1) // depth
    for i in range(rows):
        g, q = divmod(i, per)
        own_left = wide[g * hidden : (g + 1) * hidden, q * 256 : (q + 1) * 256]
        block = jnp.where(diagonal, jnp.concatenate([own_left] * fold, axis=0), 0.0).astype(BF16)
        out = jnp.dot(stack_ref[...], block, preferred_element_type=F32).astype(BF16)
        for g in range(groups):
            spread_ref[i * pair : (i + 1) * pair, g * 256 : (g + 1) * 256] = out[g * pair : (g + 1) * pair, :]
        for p in range(i * size // rows, (i + 1) * size // rows):
            relative = sum(((p >> (bits - 1 - t)) & 1) << t for t in range(bits))
            begin = pl.multiple_of((me ^ relative) * rows, rows)
            factor = inverse_ref[pl.ds(begin, rows), :]
            for h in range(rows):
                part = g_ref[h, pl.ds(begin, rows), :].astype(F32) * factor[:, h : h + 1]
                scaled_ref[p * rows : (p + 1) * rows, h * pair : (h + 1) * pair] = part.astype(BF16)


def send_kernel(scaled_ref, spread_ref, send_ref):
    half = send_ref.shape[0]
    send_ref[...] = jnp.dot(scaled_ref[half:, :], spread_ref[...], preferred_element_type=F32).astype(BF16)


def keep_kernel(rows, scaled_ref, spread_ref, x_ref, mask_ref, keep_ref, normed_ref, recip_ref, presence_ref):
    half = keep_ref.shape[0]
    keep_ref[...] = jnp.dot(scaled_ref[:half, :], spread_ref[...], preferred_element_type=F32)
    value = x_ref[...].astype(F32).T
    centered = value - jnp.mean(value, axis=0, keepdims=True)
    recip = lax.rsqrt(jnp.mean(centered * centered, axis=0, keepdims=True) + 1e-05)
    normed_ref[...] = centered * recip
    recip_ref[...] = recip
    presence_ref[...] = presence_row(own_presence(mask_ref[...], lax.axis_index("row"), rows), True)


def weigh(weight, value):
    high = value.astype(BF16)
    low = (value - high.astype(F32)).astype(BF16)
    turned = weight.astype(F32).T.astype(BF16)
    return jnp.dot(
        jnp.concatenate([turned, turned], axis=1), jnp.concatenate([high, low], axis=0), preferred_element_type=F32
    )


def outer_kernel(rows, near_ref, far_ref, scaled_ref, outer_ref, turned):
    hidden, count, pair = outer_ref.shape
    depth = count // rows
    half = near_ref.shape[0]
    turned[:, :half] = near_ref[...].T
    turned[:, half:] = far_ref[...].T
    for q in range(rows // 2):
        out = jnp.dot(
            turned[...], scaled_ref[:, q * 2 * pair : (q + 1) * 2 * pair], preferred_element_type=F32
        ).astype(BF16)
        for h in range(2):
            i = 2 * q + h
            outer_ref[:, i * depth : (i + 1) * depth, :] = out[:, h * pair : (h + 1) * pair].reshape(hidden, depth, pair)


def left_kernel(rows, outer_ref, owp_ref, lw_ref, grad_ref, total):
    hidden = lw_ref.shape[0]
    count = total.shape[0]
    depth = count // rows
    acc = jnp.zeros((count, hidden), F32)
    for e in range(0, hidden, 2):
        lhs = jnp.concatenate([outer_ref[e], outer_ref[e + 1]], axis=1)
        rhs = jnp.concatenate(
            [owp_ref[e * hidden : (e + 1) * hidden, :], owp_ref[(e + 1) * hidden : (e + 2) * hidden, :]], axis=1
        )
        acc = acc + lax.dot_general(lhs, rhs, NT, preferred_element_type=F32)
    total[...] = acc
    by_sequence = jnp.concatenate([total[pl.ds(s, rows, stride=depth), :] for s in range(depth)], axis=0)
    grad_ref[...] = weigh(lw_ref[...], by_sequence.T)


def final_kernel(rows, keep_ref, *refs):
    *got_refs, rw_ref, grad_ref, normed_ref, recip_ref, presence_ref, out_ref, flat, lanes = refs
    hidden = rw_ref.shape[0]
    depth = keep_ref.shape[1] // hidden
    total = keep_ref[...]
    for got_ref in got_refs:
        total = total + got_ref[...].astype(F32)
    flat[...] = total.T
    for s in range(depth):
        lanes[:, s * rows : (s + 1) * rows] = flat[pl.ds(s, hidden, stride=depth), :]
    grad = (weigh(rw_ref[...], lanes[...]) + grad_ref[...]) * presence_ref[...]
    normed = normed_ref[...]
    mean = jnp.mean(grad, axis=0, keepdims=True)
    cross = jnp.mean(grad * normed, axis=0, keepdims=True)
    out_ref[...] = (recip_ref[...] * (grad - mean - normed * cross)).T


def near_shape(dims, dtype):
    return pltpu.VMEM(dims, dtype)


def near(value):
    return pltpu.with_memory_space_constraint(value, pltpu.VMEM)


def far(value):
    return pltpu.with_memory_space_constraint(value, pltpu.HBM)


def call(kernel, name, out_shape, args, scratch=(), flops=0, in_specs=None):
    vmem = pl.BlockSpec(memory_space=pltpu.VMEM)
    out_specs = (vmem,) * len(out_shape) if isinstance(out_shape, tuple) else vmem
    return pl.pallas_call(
        kernel,
        out_shape=out_shape,
        in_specs=in_specs or [vmem] * len(args),
        out_specs=out_specs,
        scratch_shapes=scratch,
        compiler_params=PARAMS,
        cost_estimate=pl.CostEstimate(flops=flops, bytes_accessed=1 << 20, transcendentals=0),
        name=name,
    )(*args)


def shards(size, x, mask, residue_mask, lw, rw, ow, g):
    depth, rows, channels = x.shape
    hidden = lw.shape[1]
    width, pair = g.shape[1:]
    count = depth * rows
    flat_width = depth * hidden

    def exchange(value, bit):
        return lax.ppermute(value, "row", [(d, d ^ bit) for d in range(size)])

    sources = (x.reshape(count, channels), mask, residue_mask.reshape(1, width), lw.T, rw.T, ow, g)
    left, right, x, mask, lw, rw, owp, stack, inverse, g = call(
        functools.partial(project_kernel, rows),
        "project",
        (
            near_shape((hidden, count), BF16),
            near_shape((rows, flat_width), BF16),
            near_shape((count, channels), BF16),
            near_shape(mask.shape, mask.dtype),
            near_shape((hidden, channels), BF16),
            near_shape((hidden, channels), BF16),
            near_shape(ow.shape, BF16),
            near_shape((ow.shape[0] // 256 * pair, 256), BF16),
            near_shape((width, rows), F32),
            near_shape(g.shape, BF16),
        ),
        [far(v) for v in sources],
        [
            pltpu.VMEM((1, width), residue_mask.dtype),
            pltpu.VMEM(ow.shape, BF16),
            pltpu.VMEM((count, channels), F32),
            pltpu.VMEM((flat_width, rows), F32),
            pltpu.VMEM(ow.shape, F32),
            pltpu.SemaphoreType.DMA((len(sources),)),
        ],
        in_specs=[pl.BlockSpec(memory_space=pl.ANY)] * len(sources),
    )
    bits = [1 << t for t in range(size.bit_length() - 1)]
    stages = [bits[t : t + 2] for t in range(1, len(bits), 2)]

    def partners(stage):
        found = [0]
        for bit in reversed(stage):
            found = found + [bit ^ f for f in found]
        return found

    def parts(total, stage):
        return [piece.astype(BF16) for piece in jnp.split(total, 1 << len(stage))]

    block = right
    for stage in stages[:0:-1]:
        block = [block] + [exchange(block, other) for other in partners(stage)[1:]]
        block = jnp.concatenate(block, axis=0)
    scaled, spread = call(
        functools.partial(spread_kernel, rows, size),
        "spread",
        (near_shape((width, rows * pair), BF16), near_shape((rows * pair, flat_width), BF16)),
        [near(v) for v in (g, inverse, left, stack)],
        flops=2 * 2**30,
    )
    send = call(
        send_kernel,
        "send",
        near_shape((width // 2, flat_width), BF16),
        [near(scaled), near(spread)],
        flops=2**30,
    )
    scaled_again, send, block = lax.optimization_barrier((scaled, send, block))
    got = exchange(send, bits[0])
    keep, normed, recip, presence = call(
        functools.partial(keep_kernel, rows),
        "keep",
        (
            near_shape((width // 2, flat_width), F32),
            near_shape((channels, count), F32),
            near_shape((1, count), F32),
            near_shape((1, count), F32),
        ),
        [near(v) for v in (scaled_again, spread, x, mask)],
        flops=2**30,
    )
    total = keep + got.astype(F32)
    sums = parts(total, stages[0])
    joint = [
        exchange(jnp.concatenate([piece, block], axis=0), other) for piece, other in zip(sums[1:], partners(stages[0])[1:])
    ]
    cut = sums[0].shape[0]
    near_block = jnp.concatenate([block] + [v[cut:] for v in joint], axis=0)
    far_block = exchange(near_block, bits[0])
    keep, got = total[:cut], [v[:cut] for v in joint]
    for stage in stages[1:]:
        total = keep + sum(v.astype(F32) for v in got)
        sums = parts(total, stage)
        keep = total[: sums[0].shape[0]]
        got = [exchange(piece, other) for piece, other in zip(sums[1:], partners(stage)[1:])]
    outer = call(
        functools.partial(outer_kernel, rows),
        "outer",
        near_shape((hidden, count, pair), BF16),
        [near(v) for v in (near_block, far_block, scaled)],
        [pltpu.VMEM((flat_width, width), BF16)],
        flops=2**26,
    )
    grad = call(
        functools.partial(left_kernel, rows),
        "left",
        near_shape((channels, count), F32),
        [near(v) for v in (outer, owp, lw)],
        [pltpu.VMEM((count, hidden), F32)],
        flops=2**26,
    )
    out = call(
        functools.partial(final_kernel, rows),
        "final",
        jax.ShapeDtypeStruct((count, channels), F32),
        [near(v) for v in (keep, *got, rw, grad, normed, recip, presence)],
        [pltpu.VMEM((flat_width, rows), F32), pltpu.VMEM((hidden, count), F32)],
    )
    return out.reshape(depth, rows, channels)


def solution(mesh):
    return jax.shard_map(
        functools.partial(shards, mesh.shape["row"]),
        mesh=mesh,
        in_specs=(
            P("groups", "row", None),
            P("groups", None),
            P("groups"),
            P(),
            P(),
            P(),
            P(("groups", "row"), None, None),
        ),
        out_specs=P("groups", "row", None),
        check_vma=False,
    )
```

```python
import functools

import jax
import jax.numpy as jnp
from jax import lax
from jax.experimental import pallas as pl
from jax.experimental.pallas import tpu as pltpu
from jax.sharding import PartitionSpec as P

F32 = jnp.float32
BF16 = jnp.bfloat16
NT = (((1,), (1,)), ((), ()))
PARAMS = pltpu.CompilerParams(vmem_limit_bytes=24 * 1024 * 1024)


def iota(shape, axis):
    return lax.broadcasted_iota(jnp.int32, shape, axis)


def own_presence(mask, me, rows):
    pick = iota((mask.shape[1], rows), 0) == me * rows + iota((mask.shape[1], rows), 1)
    return jnp.dot(mask.astype(F32).astype(BF16), pick.astype(F32).astype(BF16), preferred_element_type=F32)


def presence_row(own):
    depth, rows = own.shape
    count = depth * rows
    spread = (iota((rows, count), 1) // depth == iota((rows, count), 0)).astype(F32).astype(BF16)
    wide = jnp.dot(own.astype(BF16), spread, preferred_element_type=F32)
    return jnp.sum(
        jnp.where(iota((depth, count), 1) % depth == iota((depth, count), 0), wide, 0.0), axis=0, keepdims=True
    )


def by_residue(wide_ref, rows):
    depth = wide_ref.shape[0] // rows
    return jnp.concatenate([wide_ref[pl.ds(i, depth, stride=rows), :] for i in range(rows)], axis=0)


def project_kernel(
    rows,
    x_far, mask_far, res_far, lw_far, rw_far, ow_far, g_far,
    left_ref, right_ref, x_ref, mask_ref, lw_ref, rw_ref, owp_ref, stack_ref, inverse_ref, g_ref,
    res_ref, ow_ref, normed, flat, ow_wide, arrived,
):
    sources = (x_far, mask_far, res_far, lw_far, rw_far, ow_far, g_far)
    targets = (x_ref, mask_ref, res_ref, lw_ref, rw_ref, ow_ref, g_ref)
    copies = [pltpu.make_async_copy(a, b, arrived.at[t]) for t, (a, b) in enumerate(zip(sources, targets))]
    for copy in copies:
        copy.start()
    for copy in copies[:-1]:
        copy.wait()
    count, channels = x_ref.shape
    depth, width = mask_ref.shape
    hidden = lw_ref.shape[0]
    pair = ow_ref.shape[1]
    me = lax.axis_index("row")
    value = x_ref[...].astype(F32)
    centered = value - jnp.mean(value, axis=-1, keepdims=True)
    recip = lax.rsqrt(jnp.mean(centered * centered, axis=-1, keepdims=True) + 1e-05)
    value = centered * recip
    normed[...] = value
    own = own_presence(mask_ref[...], me, rows)
    weights = jnp.concatenate([lw_ref[...], rw_ref[...]], axis=0)
    both = lax.dot_general(weights, by_residue(normed, rows).astype(BF16), NT, preferred_element_type=F32)
    both = both * presence_row(own)
    left_ref[...] = both[:hidden].astype(BF16)
    for j in range(rows):
        flat[j * hidden : (j + 1) * hidden, :] = both[hidden:, j * depth : (j + 1) * depth]
    right_ref[...] = jnp.concatenate(
        [flat[pl.ds(e, rows, stride=hidden), :] for e in range(hidden)], axis=1
    ).astype(BF16)
    mask = mask_ref[...].astype(F32)
    residue = res_ref[...].astype(F32)
    residue_own = own_presence(jnp.broadcast_to(res_ref[...], (8, width)), me, rows)[:1]
    tall = jnp.concatenate([mask, jnp.broadcast_to(residue, (8, width))], axis=0).T
    counts = jnp.dot(tall[:, :depth].astype(BF16), own.astype(BF16), preferred_element_type=F32) + 0.001
    inverse_ref[...] = tall[:, depth : depth + 1] * residue_own / counts
    ow_wide[...] = ow_ref[...].astype(F32)
    for e in range(hidden):
        owp_ref[e * hidden : (e + 1) * hidden, :] = ow_wide[pl.ds(e, hidden, stride=hidden), :].astype(BF16)
    for g in range(hidden * hidden // 256):
        stack_ref[g * pair : (g + 1) * pair, :] = owp_ref[g * 256 : (g + 1) * 256, :].T
    copies[-1].wait()


def spread_kernel(rows, size, g_ref, inverse_ref, left_ref, stack_ref, scaled_ref, spread_ref):
    hidden, count = left_ref.shape
    depth = count // rows
    pair = g_ref.shape[2]
    me = lax.axis_index("row")
    bits = size.bit_length() - 1
    fold = 256 // hidden
    groups = hidden // fold
    per = 128 // depth
    blocks = rows // per
    tile = jnp.concatenate([left_ref[:, g * 128 : (g + 1) * 128] for g in range(blocks)], axis=0)
    column = iota((128, per * 256), 1)
    repeat = (column % depth + depth * (column // 256)) == iota((128, per * 256), 0)
    wide = jnp.dot(tile, repeat.astype(F32).astype(BF16), preferred_element_type=F32)
    diagonal = iota((256, 256), 0) // hidden == iota((256, 256), 1) // depth
    for i in range(rows):
        g, q = divmod(i, per)
        own_left = wide[g * hidden : (g + 1) * hidden, q * 256 : (q + 1) * 256]
        block = jnp.where(diagonal, jnp.concatenate([own_left] * fold, axis=0), 0.0).astype(BF16)
        out = jnp.dot(stack_ref[...], block, preferred_element_type=F32).astype(BF16)
        for g in range(groups):
            spread_ref[i * pair : (i + 1) * pair, g * 256 : (g + 1) * 256] = out[g * pair : (g + 1) * pair, :]
        for p in range(i * size // rows, (i + 1) * size // rows):
            relative = sum(((p >> (bits - 1 - t)) & 1) << t for t in range(bits))
            begin = pl.multiple_of((me ^ relative) * rows, rows)
            factor = inverse_ref[pl.ds(begin, rows), :]
            for h in range(rows):
                part = g_ref[h, pl.ds(begin, rows), :].astype(F32) * factor[:, h : h + 1]
                scaled_ref[p * rows : (p + 1) * rows, h * pair : (h + 1) * pair] = part.astype(BF16)


def send_kernel(scaled_ref, spread_ref, send_ref):
    half = send_ref.shape[0]
    send_ref[...] = jnp.dot(scaled_ref[half:, :], spread_ref[...], preferred_element_type=F32).astype(BF16)


def keep_kernel(
    rows, scaled_ref, spread_ref, x_ref, mask_ref, keep_ref, normed_ref, recip_ref, presence_ref, wide
):
    half = keep_ref.shape[0]
    keep_ref[...] = jnp.dot(scaled_ref[:half, :], spread_ref[...], preferred_element_type=F32)
    wide[...] = x_ref[...].astype(F32)
    value = by_residue(wide, rows).T
    centered = value - jnp.mean(value, axis=0, keepdims=True)
    recip = lax.rsqrt(jnp.mean(centered * centered, axis=0, keepdims=True) + 1e-05)
    normed_ref[...] = centered * recip
    recip_ref[...] = recip
    presence_ref[...] = presence_row(own_presence(mask_ref[...], lax.axis_index("row"), rows))


def weigh(weight, value):
    high = value.astype(BF16)
    low = (value - high.astype(F32)).astype(BF16)
    turned = weight.astype(F32).T.astype(BF16)
    return jnp.dot(
        jnp.concatenate([turned, turned], axis=1), jnp.concatenate([high, low], axis=0), preferred_element_type=F32
    )


def outer_kernel(rows, near_ref, far_ref, scaled_ref, outer_ref, turned):
    hidden, count, pair = outer_ref.shape
    depth = count // rows
    half = near_ref.shape[0]
    turned[:, :half] = near_ref[...].T
    turned[:, half:] = far_ref[...].T
    for q in range(rows // 2):
        out = jnp.dot(
            turned[...], scaled_ref[:, q * 2 * pair : (q + 1) * 2 * pair], preferred_element_type=F32
        ).astype(BF16)
        for h in range(2):
            i = 2 * q + h
            outer_ref[:, i * depth : (i + 1) * depth, :] = out[:, h * pair : (h + 1) * pair].reshape(hidden, depth, pair)


def left_kernel(outer_ref, owp_ref, lw_ref, grad_ref):
    hidden, count, _ = outer_ref.shape
    acc = jnp.zeros((count, hidden), F32)
    for e in range(0, hidden, 2):
        lhs = jnp.concatenate([outer_ref[e], outer_ref[e + 1]], axis=1)
        rhs = jnp.concatenate(
            [owp_ref[e * hidden : (e + 1) * hidden, :], owp_ref[(e + 1) * hidden : (e + 2) * hidden, :]], axis=1
        )
        acc = acc + lax.dot_general(lhs, rhs, NT, preferred_element_type=F32)
    grad_ref[...] = weigh(lw_ref[...], acc.T)


def final_kernel(rows, keep_ref, *refs):
    *got_refs, rw_ref, grad_ref, normed_ref, recip_ref, presence_ref, out_ref, flat = refs
    hidden = rw_ref.shape[0]
    depth = keep_ref.shape[1] // hidden
    total = keep_ref[...]
    for got_ref in got_refs:
        total = total + got_ref[...].astype(F32)
    for e in range(hidden):
        flat[pl.ds(e, rows, stride=hidden), :] = total[:, e * depth : (e + 1) * depth]
    right = jnp.concatenate([flat[j * hidden : (j + 1) * hidden, :] for j in range(rows)], axis=1)
    grad = (weigh(rw_ref[...], right) + grad_ref[...]) * presence_ref[...]
    normed = normed_ref[...]
    mean = jnp.mean(grad, axis=0, keepdims=True)
    cross = jnp.mean(grad * normed, axis=0, keepdims=True)
    out = (recip_ref[...] * (grad - mean - normed * cross)).T
    for i in range(rows):
        out_ref[pl.ds(i, depth, stride=rows), :] = out[i * depth : (i + 1) * depth, :]


def near_shape(dims, dtype):
    return pltpu.VMEM(dims, dtype)


def near(value):
    return pltpu.with_memory_space_constraint(value, pltpu.VMEM)


def far(value):
    return pltpu.with_memory_space_constraint(value, pltpu.HBM)


def call(kernel, name, out_shape, args, scratch=(), flops=0, in_specs=None):
    vmem = pl.BlockSpec(memory_space=pltpu.VMEM)
    out_specs = (vmem,) * len(out_shape) if isinstance(out_shape, tuple) else vmem
    return pl.pallas_call(
        kernel,
        out_shape=out_shape,
        in_specs=in_specs or [vmem] * len(args),
        out_specs=out_specs,
        scratch_shapes=scratch,
        compiler_params=PARAMS,
        cost_estimate=pl.CostEstimate(flops=flops, bytes_accessed=1 << 20, transcendentals=0),
        name=name,
    )(*args)


def shards(size, x, mask, residue_mask, lw, rw, ow, g):
    depth, rows, channels = x.shape
    hidden = lw.shape[1]
    width, pair = g.shape[1:]
    count = depth * rows
    flat_width = depth * hidden

    def exchange(value, bit):
        return lax.ppermute(value, "row", [(d, d ^ bit) for d in range(size)])

    sources = (x.reshape(count, channels), mask, residue_mask.reshape(1, width), lw.T, rw.T, ow, g)
    left, right, x, mask, lw, rw, owp, stack, inverse, g = call(
        functools.partial(project_kernel, rows),
        "project",
        (
            near_shape((hidden, count), BF16),
            near_shape((rows, flat_width), BF16),
            near_shape((count, channels), BF16),
            near_shape(mask.shape, mask.dtype),
            near_shape((hidden, channels), BF16),
            near_shape((hidden, channels), BF16),
            near_shape(ow.shape, BF16),
            near_shape((ow.shape[0] // 256 * pair, 256), BF16),
            near_shape((width, rows), F32),
            near_shape(g.shape, BF16),
        ),
        [far(v) for v in sources],
        [
            pltpu.VMEM((1, width), residue_mask.dtype),
            pltpu.VMEM(ow.shape, BF16),
            pltpu.VMEM((count, channels), F32),
            pltpu.VMEM((rows * hidden, depth), F32),
            pltpu.VMEM(ow.shape, F32),
            pltpu.SemaphoreType.DMA((len(sources),)),
        ],
        in_specs=[pl.BlockSpec(memory_space=pl.ANY)] * len(sources),
    )
    bits = [1 << t for t in range(size.bit_length() - 1)]
    stages = [bits[t : t + 2] for t in range(1, len(bits), 2)]

    def partners(stage):
        found = [0]
        for bit in reversed(stage):
            found = found + [bit ^ f for f in found]
        return found

    def parts(total, stage):
        return [piece.astype(BF16) for piece in jnp.split(total, 1 << len(stage))]

    block = right
    for stage in stages[:0:-1]:
        block = [block] + [exchange(block, other) for other in partners(stage)[1:]]
        block = jnp.concatenate(block, axis=0)
    scaled, spread = call(
        functools.partial(spread_kernel, rows, size),
        "spread",
        (near_shape((width, rows * pair), BF16), near_shape((rows * pair, flat_width), BF16)),
        [near(v) for v in (g, inverse, left, stack)],
        flops=2 * 2**30,
    )
    send = call(
        send_kernel,
        "send",
        near_shape((width // 2, flat_width), BF16),
        [near(scaled), near(spread)],
        flops=2**30,
    )
    scaled_again, send, block = lax.optimization_barrier((scaled, send, block))
    got = exchange(send, bits[0])
    keep, normed, recip, presence = call(
        functools.partial(keep_kernel, rows),
        "keep",
        (
            near_shape((width // 2, flat_width), F32),
            near_shape((channels, count), F32),
            near_shape((1, count), F32),
            near_shape((1, count), F32),
        ),
        [near(v) for v in (scaled_again, spread, x, mask)],
        [pltpu.VMEM((count, channels), F32)],
        flops=2**30,
    )
    total = keep + got.astype(F32)
    sums = parts(total, stages[0])
    joint = [
        exchange(jnp.concatenate([piece, block], axis=0), other) for piece, other in zip(sums[1:], partners(stages[0])[1:])
    ]
    cut = sums[0].shape[0]
    near_block = jnp.concatenate([block] + [v[cut:] for v in joint], axis=0)
    far_block = exchange(near_block, bits[0])
    keep, got = total[:cut], [v[:cut] for v in joint]
    for stage in stages[1:]:
        total = keep + sum(v.astype(F32) for v in got)
        sums = parts(total, stage)
        keep = total[: sums[0].shape[0]]
        got = [exchange(piece, other) for piece, other in zip(sums[1:], partners(stage)[1:])]
    outer = call(
        functools.partial(outer_kernel, rows),
        "outer",
        near_shape((hidden, count, pair), BF16),
        [near(v) for v in (near_block, far_block, scaled)],
        [pltpu.VMEM((flat_width, width), BF16)],
        flops=2**26,
    )
    grad = call(
        left_kernel,
        "left",
        near_shape((channels, count), F32),
        [near(v) for v in (outer, owp, lw)],
        flops=2**26,
    )
    out = call(
        functools.partial(final_kernel, rows),
        "final",
        jax.ShapeDtypeStruct((count, channels), F32),
        [near(v) for v in (keep, *got, rw, grad, normed, recip, presence)],
        [pltpu.VMEM((rows * hidden, depth), F32)],
    )
    return out.reshape(depth, rows, channels)


def solution(mesh):
    return jax.shard_map(
        functools.partial(shards, mesh.shape["row"]),
        mesh=mesh,
        in_specs=(
            P("groups", "row", None),
            P("groups", None),
            P("groups"),
            P(),
            P(),
            P(),
            P(("groups", "row"), None, None),
        ),
        out_specs=P("groups", "row", None),
        check_vma=False,
    )
```

```python
import functools

import jax
import jax.numpy as jnp
from jax import lax
from jax.experimental import pallas as pl
from jax.experimental.pallas import tpu as pltpu
from jax.sharding import PartitionSpec as P

F32 = jnp.float32
BF16 = jnp.bfloat16
NT = (((1,), (1,)), ((), ()))
PARAMS = pltpu.CompilerParams(vmem_limit_bytes=24 * 1024 * 1024)


def iota(shape, axis):
    return lax.broadcasted_iota(jnp.int32, shape, axis)


def bits_of(condition):
    return condition.astype(F32).astype(BF16)


def by_residue(wide_ref, rows):
    depth = wide_ref.shape[0] // rows
    return jnp.concatenate([wide_ref[pl.ds(i, depth, stride=rows), :] for i in range(rows)], axis=0)


def project_kernel(
    rows,
    x_far, mask_far, res_far, lw_far, rw_far, ow_far, g_far,
    left_ref, right_ref, x_ref, presence_ref, lw_ref, rw_ref, owp_ref, stack_ref, inverse_ref, g_ref,
    repeat_ref, diagonal_ref,
    mask_ref, res_ref, ow_ref, normed, flat, ow_wide, pick, along, arrived,
):
    sources = (x_far, mask_far, res_far, lw_far, rw_far, ow_far, g_far)
    targets = (x_ref, mask_ref, res_ref, lw_ref, rw_ref, ow_ref, g_ref)
    copies = [pltpu.make_async_copy(a, b, arrived.at[t]) for t, (a, b) in enumerate(zip(sources, targets))]
    for copy in copies:
        copy.start()
    count, channels = x_ref.shape
    depth, width = mask_ref.shape
    hidden = lw_ref.shape[0]
    pair = ow_ref.shape[1]
    me = lax.axis_index("row")
    pick[...] = bits_of(iota((width, rows), 0) == me * rows + iota((width, rows), 1))
    along[...] = bits_of(iota((rows, count), 1) // depth == iota((rows, count), 0))
    column = iota(repeat_ref.shape, 1)
    repeat_ref[...] = bits_of((column % depth + depth * (column // 256)) == iota(repeat_ref.shape, 0))
    diagonal_ref[...] = bits_of(iota((256, 256), 0) // hidden == iota((256, 256), 1) // depth)
    for copy in copies[:-1]:
        copy.wait()
    value = x_ref[...].astype(F32)
    centered = value - jnp.mean(value, axis=-1, keepdims=True)
    recip = lax.rsqrt(jnp.mean(centered * centered, axis=-1, keepdims=True) + 1e-05)
    value = centered * recip
    normed[...] = value
    flags = jnp.concatenate(
        [mask_ref[...].astype(F32), jnp.broadcast_to(res_ref[...].astype(F32), (8, width))], axis=0
    )
    own = jnp.dot(flags.astype(BF16), pick[...], preferred_element_type=F32)
    wide = jnp.dot(own[:depth].astype(BF16), along[...], preferred_element_type=F32)
    same = iota((depth, count), 1) % depth == iota((depth, count), 0)
    presence = jnp.sum(jnp.where(same, wide, 0.0), axis=0, keepdims=True)
    presence_ref[...] = presence
    weights = jnp.concatenate([lw_ref[...], rw_ref[...]], axis=0)
    both = lax.dot_general(weights, by_residue(normed, rows).astype(BF16), NT, preferred_element_type=F32)
    both = both * presence
    left_ref[...] = both[:hidden].astype(BF16)
    for j in range(rows):
        flat[j * hidden : (j + 1) * hidden, :] = both[hidden:, j * depth : (j + 1) * depth]
    right_ref[...] = jnp.concatenate(
        [flat[pl.ds(e, rows, stride=hidden), :] for e in range(hidden)], axis=1
    ).astype(BF16)
    tall = flags.T
    counts = jnp.dot(tall[:, :depth].astype(BF16), own[:depth].astype(BF16), preferred_element_type=F32) + 0.001
    inverse_ref[...] = tall[:, depth : depth + 1] * own[depth : depth + 1] / counts
    ow_wide[...] = ow_ref[...].astype(F32)
    for e in range(hidden):
        owp_ref[e * hidden : (e + 1) * hidden, :] = ow_wide[pl.ds(e, hidden, stride=hidden), :].astype(BF16)
    for g in range(hidden * hidden // 256):
        stack_ref[g * pair : (g + 1) * pair, :] = owp_ref[g * 256 : (g + 1) * 256, :].T
    copies[-1].wait()


def spread_kernel(
    rows, size, g_ref, inverse_ref, left_ref, stack_ref, repeat_ref, diagonal_ref, scaled_ref, spread_ref
):
    hidden, count = left_ref.shape
    depth = count // rows
    pair = g_ref.shape[2]
    me = lax.axis_index("row")
    bits = size.bit_length() - 1
    fold = 256 // hidden
    groups = hidden // fold
    per = 128 // depth
    blocks = rows // per
    tile = jnp.concatenate([left_ref[:, g * 128 : (g + 1) * 128] for g in range(blocks)], axis=0)
    wide = jnp.dot(tile, repeat_ref[...], preferred_element_type=F32).astype(BF16)
    for i in range(rows):
        g, q = divmod(i, per)
        own_left = wide[g * hidden : (g + 1) * hidden, q * 256 : (q + 1) * 256]
        block = jnp.concatenate([own_left] * fold, axis=0) * diagonal_ref[...]
        out = jnp.dot(stack_ref[...], block, preferred_element_type=F32).astype(BF16)
        for g in range(groups):
            spread_ref[i * pair : (i + 1) * pair, g * 256 : (g + 1) * 256] = out[g * pair : (g + 1) * pair, :]
        for p in range(i * size // rows, (i + 1) * size // rows):
            relative = sum(((p >> (bits - 1 - t)) & 1) << t for t in range(bits))
            begin = pl.multiple_of((me ^ relative) * rows, rows)
            factor = inverse_ref[pl.ds(begin, rows), :]
            for h in range(rows):
                part = g_ref[h, pl.ds(begin, rows), :].astype(F32) * factor[:, h : h + 1]
                scaled_ref[p * rows : (p + 1) * rows, h * pair : (h + 1) * pair] = part.astype(BF16)


def send_kernel(scaled_ref, spread_ref, send_ref):
    half = send_ref.shape[0]
    send_ref[...] = jnp.dot(scaled_ref[half:, :], spread_ref[...], preferred_element_type=F32).astype(BF16)


def keep_kernel(
    rows, scaled_ref, spread_ref, x_ref, keep_ref, normed_ref, recip_ref, wide
):
    half = keep_ref.shape[0]
    keep_ref[...] = jnp.dot(scaled_ref[:half, :], spread_ref[...], preferred_element_type=F32)
    wide[...] = x_ref[...].astype(F32)
    value = by_residue(wide, rows).T
    centered = value - jnp.mean(value, axis=0, keepdims=True)
    recip = lax.rsqrt(jnp.mean(centered * centered, axis=0, keepdims=True) + 1e-05)
    normed_ref[...] = centered * recip
    recip_ref[...] = recip


def weigh(weight, value):
    high = value.astype(BF16)
    low = (value - high.astype(F32)).astype(BF16)
    turned = weight.astype(F32).T.astype(BF16)
    return jnp.dot(
        jnp.concatenate([turned, turned], axis=1), jnp.concatenate([high, low], axis=0), preferred_element_type=F32
    )


def outer_kernel(rows, near_ref, far_ref, scaled_ref, outer_ref, turned):
    hidden, count, pair = outer_ref.shape
    depth = count // rows
    half = near_ref.shape[0]
    turned[:, :half] = near_ref[...].T
    turned[:, half:] = far_ref[...].T
    for q in range(rows // 2):
        out = jnp.dot(
            turned[...], scaled_ref[:, q * 2 * pair : (q + 1) * 2 * pair], preferred_element_type=F32
        ).astype(BF16)
        for h in range(2):
            i = 2 * q + h
            outer_ref[:, i * depth : (i + 1) * depth, :] = out[:, h * pair : (h + 1) * pair].reshape(hidden, depth, pair)


def left_kernel(outer_ref, owp_ref, lw_ref, grad_ref):
    hidden, count, _ = outer_ref.shape
    acc = jnp.zeros((count, hidden), F32)
    for e in range(0, hidden, 2):
        lhs = jnp.concatenate([outer_ref[e], outer_ref[e + 1]], axis=1)
        rhs = jnp.concatenate(
            [owp_ref[e * hidden : (e + 1) * hidden, :], owp_ref[(e + 1) * hidden : (e + 2) * hidden, :]], axis=1
        )
        acc = acc + lax.dot_general(lhs, rhs, NT, preferred_element_type=F32)
    grad_ref[...] = weigh(lw_ref[...], acc.T)


def final_kernel(rows, keep_ref, *refs):
    *got_refs, rw_ref, grad_ref, normed_ref, recip_ref, presence_ref, out_ref, flat = refs
    hidden = rw_ref.shape[0]
    depth = keep_ref.shape[1] // hidden
    total = keep_ref[...]
    for got_ref in got_refs:
        total = total + got_ref[...].astype(F32)
    for e in range(hidden):
        flat[pl.ds(e, rows, stride=hidden), :] = total[:, e * depth : (e + 1) * depth]
    right = jnp.concatenate([flat[j * hidden : (j + 1) * hidden, :] for j in range(rows)], axis=1)
    grad = (weigh(rw_ref[...], right) + grad_ref[...]) * presence_ref[...]
    normed = normed_ref[...]
    mean = jnp.mean(grad, axis=0, keepdims=True)
    cross = jnp.mean(grad * normed, axis=0, keepdims=True)
    out = (recip_ref[...] * (grad - mean - normed * cross)).T
    for i in range(rows):
        out_ref[pl.ds(i, depth, stride=rows), :] = out[i * depth : (i + 1) * depth, :]


def near_shape(dims, dtype):
    return pltpu.VMEM(dims, dtype)


def near(value):
    return pltpu.with_memory_space_constraint(value, pltpu.VMEM)


def far(value):
    return pltpu.with_memory_space_constraint(value, pltpu.HBM)


def call(kernel, name, out_shape, args, scratch=(), flops=0, in_specs=None):
    vmem = pl.BlockSpec(memory_space=pltpu.VMEM)
    out_specs = (vmem,) * len(out_shape) if isinstance(out_shape, tuple) else vmem
    return pl.pallas_call(
        kernel,
        out_shape=out_shape,
        in_specs=in_specs or [vmem] * len(args),
        out_specs=out_specs,
        scratch_shapes=scratch,
        compiler_params=PARAMS,
        cost_estimate=pl.CostEstimate(flops=flops, bytes_accessed=1 << 20, transcendentals=0),
        name=name,
    )(*args)


def shards(size, x, mask, residue_mask, lw, rw, ow, g):
    depth, rows, channels = x.shape
    hidden = lw.shape[1]
    width, pair = g.shape[1:]
    count = depth * rows
    flat_width = depth * hidden

    def exchange(value, bit):
        return lax.ppermute(value, "row", [(d, d ^ bit) for d in range(size)])

    sources = (x.reshape(count, channels), mask, residue_mask.reshape(1, width), lw.T, rw.T, ow, g)
    left, right, x, presence, lw, rw, owp, stack, inverse, g, repeat, diagonal = call(
        functools.partial(project_kernel, rows),
        "project",
        (
            near_shape((hidden, count), BF16),
            near_shape((rows, flat_width), BF16),
            near_shape((count, channels), BF16),
            near_shape((1, count), F32),
            near_shape((hidden, channels), BF16),
            near_shape((hidden, channels), BF16),
            near_shape(ow.shape, BF16),
            near_shape((ow.shape[0] // 256 * pair, 256), BF16),
            near_shape((width, rows), F32),
            near_shape(g.shape, BF16),
            near_shape((128, 128 // depth * 256), BF16),
            near_shape((256, 256), BF16),
        ),
        [far(v) for v in sources],
        [
            pltpu.VMEM(mask.shape, mask.dtype),
            pltpu.VMEM((1, width), residue_mask.dtype),
            pltpu.VMEM(ow.shape, BF16),
            pltpu.VMEM((count, channels), F32),
            pltpu.VMEM((rows * hidden, depth), F32),
            pltpu.VMEM(ow.shape, F32),
            pltpu.VMEM((width, rows), BF16),
            pltpu.VMEM((rows, count), BF16),
            pltpu.SemaphoreType.DMA((len(sources),)),
        ],
        in_specs=[pl.BlockSpec(memory_space=pl.ANY)] * len(sources),
    )
    bits = [1 << t for t in range(size.bit_length() - 1)]
    stages = [bits[t : t + 2] for t in range(1, len(bits), 2)]

    def partners(stage):
        found = [0]
        for bit in reversed(stage):
            found = found + [bit ^ f for f in found]
        return found

    def parts(total, stage):
        return [piece.astype(BF16) for piece in jnp.split(total, 1 << len(stage))]

    block = right
    for stage in stages[:0:-1]:
        block = [block] + [exchange(block, other) for other in partners(stage)[1:]]
        block = jnp.concatenate(block, axis=0)
    scaled, spread = call(
        functools.partial(spread_kernel, rows, size),
        "spread",
        (near_shape((width, rows * pair), BF16), near_shape((rows * pair, flat_width), BF16)),
        [near(v) for v in (g, inverse, left, stack, repeat, diagonal)],
        flops=2 * 2**30,
    )
    send = call(
        send_kernel,
        "send",
        near_shape((width // 2, flat_width), BF16),
        [near(scaled), near(spread)],
        flops=2**30,
    )
    scaled_again, send, block = lax.optimization_barrier((scaled, send, block))
    got = exchange(send, bits[0])
    keep, normed, recip = call(
        functools.partial(keep_kernel, rows),
        "keep",
        (
            near_shape((width // 2, flat_width), F32),
            near_shape((channels, count), F32),
            near_shape((1, count), F32),
        ),
        [near(v) for v in (scaled_again, spread, x)],
        [pltpu.VMEM((count, channels), F32)],
        flops=2**30,
    )
    total = keep + got.astype(F32)
    sums = parts(total, stages[0])
    joint = [
        exchange(jnp.concatenate([piece, block], axis=0), other) for piece, other in zip(sums[1:], partners(stages[0])[1:])
    ]
    cut = sums[0].shape[0]
    keep = total[:cut]
    for v in joint[::-1]:
        keep = lax.optimization_barrier(keep + v[:cut].astype(F32))
    joint, _ = lax.optimization_barrier((joint, keep))
    near_block = jnp.concatenate([block] + [v[cut:] for v in joint], axis=0)
    far_block = exchange(near_block, bits[0])
    got = []
    for stage in stages[1:]:
        total = keep + sum(v.astype(F32) for v in got) if got else keep
        sums = parts(total, stage)
        keep = total[: sums[0].shape[0]]
        got = [exchange(piece, other) for piece, other in zip(sums[1:], partners(stage)[1:])]
    outer = call(
        functools.partial(outer_kernel, rows),
        "outer",
        near_shape((hidden, count, pair), BF16),
        [near(v) for v in (near_block, far_block, scaled)],
        [pltpu.VMEM((flat_width, width), BF16)],
        flops=2**26,
    )
    grad = call(
        left_kernel,
        "left",
        near_shape((channels, count), F32),
        [near(v) for v in (outer, owp, lw)],
        flops=2**26,
    )
    out = call(
        functools.partial(final_kernel, rows),
        "final",
        jax.ShapeDtypeStruct((count, channels), F32),
        [near(v) for v in (keep, *got, rw, grad, normed, recip, presence)],
        [pltpu.VMEM((rows * hidden, depth), F32)],
    )
    return out.reshape(depth, rows, channels)


def solution(mesh):
    return jax.shard_map(
        functools.partial(shards, mesh.shape["row"]),
        mesh=mesh,
        in_specs=(
            P("groups", "row", None),
            P("groups", None),
            P("groups"),
            P(),
            P(),
            P(),
            P(("groups", "row"), None, None),
        ),
        out_specs=P("groups", "row", None),
        check_vma=False,
    )
```

```python
import functools

import jax
import jax.numpy as jnp
from jax import lax
from jax.experimental import pallas as pl
from jax.experimental.pallas import tpu as pltpu
from jax.sharding import PartitionSpec as P

F32 = jnp.float32
BF16 = jnp.bfloat16
NT = (((1,), (1,)), ((), ()))
PARAMS = pltpu.CompilerParams(vmem_limit_bytes=24 * 1024 * 1024)


def iota(shape, axis):
    return lax.broadcasted_iota(jnp.int32, shape, axis)


def bits_of(condition):
    return condition.astype(F32).astype(BF16)


def by_residue(wide_ref, rows):
    depth = wide_ref.shape[0] // rows
    return jnp.concatenate([wide_ref[pl.ds(i, depth, stride=rows), :] for i in range(rows)], axis=0)


def project_kernel(
    rows,
    x_far, mask_far, res_far, lw_far, rw_far, ow_far, g_far,
    left_ref, right_ref, x_ref, presence_ref, lw_ref, rw_ref, owp_ref, stack_ref, inverse_ref, g_ref,
    repeat_ref, diagonal_ref,
    mask_ref, res_ref, ow_ref, normed, flat, ow_wide, pick, along, arrived,
):
    sources = (x_far, mask_far, res_far, lw_far, rw_far, ow_far, g_far)
    targets = (x_ref, mask_ref, res_ref, lw_ref, rw_ref, ow_ref, g_ref)
    copies = [pltpu.make_async_copy(a, b, arrived.at[t]) for t, (a, b) in enumerate(zip(sources, targets))]
    for copy in copies:
        copy.start()
    count, channels = x_ref.shape
    depth, width = mask_ref.shape
    hidden = lw_ref.shape[0]
    pair = ow_ref.shape[1]
    me = lax.axis_index("row")
    pick[...] = bits_of(iota((width, rows), 0) == me * rows + iota((width, rows), 1))
    along[...] = bits_of(iota((rows, count), 1) // depth == iota((rows, count), 0))
    column = iota(repeat_ref.shape, 1)
    repeat_ref[...] = bits_of((column % depth + depth * (column // 256)) == iota(repeat_ref.shape, 0))
    diagonal_ref[...] = bits_of(iota((256, 256), 0) // hidden == iota((256, 256), 1) // depth)
    for copy in copies[:-1]:
        copy.wait()
    value = x_ref[...].astype(F32)
    centered = value - jnp.mean(value, axis=-1, keepdims=True)
    recip = lax.rsqrt(jnp.mean(centered * centered, axis=-1, keepdims=True) + 1e-05)
    value = centered * recip
    normed[...] = value
    flags = jnp.concatenate(
        [mask_ref[...].astype(F32), jnp.broadcast_to(res_ref[...].astype(F32), (8, width))], axis=0
    )
    own = jnp.dot(flags.astype(BF16), pick[...], preferred_element_type=F32)
    wide = jnp.dot(own[:depth].astype(BF16), along[...], preferred_element_type=F32)
    same = iota((depth, count), 1) % depth == iota((depth, count), 0)
    presence = jnp.sum(jnp.where(same, wide, 0.0), axis=0, keepdims=True)
    presence_ref[...] = presence
    weights = jnp.concatenate([lw_ref[...], rw_ref[...]], axis=0)
    both = lax.dot_general(weights, by_residue(normed, rows).astype(BF16), NT, preferred_element_type=F32)
    both = both * presence
    left_ref[...] = both[:hidden].astype(BF16)
    for j in range(rows):
        flat[j * hidden : (j + 1) * hidden, :] = both[hidden:, j * depth : (j + 1) * depth]
    right_ref[...] = jnp.concatenate(
        [flat[pl.ds(e, rows, stride=hidden), :] for e in range(hidden)], axis=1
    ).astype(BF16)
    tall = flags.T
    counts = jnp.dot(tall[:, :depth].astype(BF16), own[:depth].astype(BF16), preferred_element_type=F32) + 0.001
    inverse_ref[...] = tall[:, depth : depth + 1] * own[depth : depth + 1] / counts
    ow_wide[...] = ow_ref[...].astype(F32)
    for e in range(hidden):
        owp_ref[e * hidden : (e + 1) * hidden, :] = ow_wide[pl.ds(e, hidden, stride=hidden), :].astype(BF16)
    for g in range(hidden * hidden // 256):
        stack_ref[g * pair : (g + 1) * pair, :] = owp_ref[g * 256 : (g + 1) * 256, :].T
    copies[-1].wait()


def spread_kernel(
    rows, size, g_ref, inverse_ref, left_ref, stack_ref, repeat_ref, diagonal_ref, scaled_ref, spread_ref
):
    hidden, count = left_ref.shape
    depth = count // rows
    pair = g_ref.shape[2]
    me = lax.axis_index("row")
    bits = size.bit_length() - 1
    fold = 256 // hidden
    groups = hidden // fold
    per = 128 // depth
    blocks = rows // per
    tile = jnp.concatenate([left_ref[:, g * 128 : (g + 1) * 128] for g in range(blocks)], axis=0)
    wide = jnp.dot(tile, repeat_ref[...], preferred_element_type=F32).astype(BF16)
    for i in range(rows):
        g, q = divmod(i, per)
        own_left = wide[g * hidden : (g + 1) * hidden, q * 256 : (q + 1) * 256]
        block = jnp.concatenate([own_left] * fold, axis=0) * diagonal_ref[...]
        out = jnp.dot(stack_ref[...], block, preferred_element_type=F32).astype(BF16)
        for g in range(groups):
            spread_ref[i * pair : (i + 1) * pair, g * 256 : (g + 1) * 256] = out[g * pair : (g + 1) * pair, :]
        for p in range(i * size // rows, (i + 1) * size // rows):
            relative = sum(((p >> (bits - 1 - t)) & 1) << t for t in range(bits))
            begin = pl.multiple_of((me ^ relative) * rows, rows)
            factor = inverse_ref[pl.ds(begin, rows), :]
            for h in range(rows):
                part = g_ref[h, pl.ds(begin, rows), :].astype(F32) * factor[:, h : h + 1]
                scaled_ref[p * rows : (p + 1) * rows, h * pair : (h + 1) * pair] = part.astype(BF16)


def send_kernel(scaled_ref, spread_ref, send_ref):
    half = send_ref.shape[0]
    send_ref[...] = jnp.dot(scaled_ref[half:, :], spread_ref[...], preferred_element_type=F32).astype(BF16)


def keep_kernel(
    rows, scaled_ref, spread_ref, x_ref, keep_ref, normed_ref, recip_ref, wide
):
    half = keep_ref.shape[0]
    keep_ref[...] = jnp.dot(scaled_ref[:half, :], spread_ref[...], preferred_element_type=F32)
    wide[...] = x_ref[...].astype(F32)
    value = by_residue(wide, rows).T
    centered = value - jnp.mean(value, axis=0, keepdims=True)
    recip = lax.rsqrt(jnp.mean(centered * centered, axis=0, keepdims=True) + 1e-05)
    normed_ref[...] = centered * recip
    recip_ref[...] = recip


def weigh(weight, value):
    high = value.astype(BF16)
    low = (value - high.astype(F32)).astype(BF16)
    turned = weight.astype(F32).T.astype(BF16)
    return jnp.dot(
        jnp.concatenate([turned, turned], axis=1), jnp.concatenate([high, low], axis=0), preferred_element_type=F32
    )


def outer_kernel(rows, near_ref, far_ref, scaled_ref, outer_ref, turned):
    hidden, count, pair = outer_ref.shape
    depth = count // rows
    half = near_ref.shape[0]
    turned[:, :half] = near_ref[...].T
    turned[:, half:] = far_ref[...].T
    for q in range(rows // 2):
        out = jnp.dot(
            turned[...], scaled_ref[:, q * 2 * pair : (q + 1) * 2 * pair], preferred_element_type=F32
        ).astype(BF16)
        for h in range(2):
            i = 2 * q + h
            outer_ref[:, i * depth : (i + 1) * depth, :] = out[:, h * pair : (h + 1) * pair].reshape(hidden, depth, pair)


def left_kernel(outer_ref, owp_ref, lw_ref, grad_ref):
    hidden, count, _ = outer_ref.shape
    acc = jnp.zeros((count, hidden), F32)
    for e in range(0, hidden, 2):
        lhs = jnp.concatenate([outer_ref[e], outer_ref[e + 1]], axis=1)
        rhs = jnp.concatenate(
            [owp_ref[e * hidden : (e + 1) * hidden, :], owp_ref[(e + 1) * hidden : (e + 2) * hidden, :]], axis=1
        )
        acc = acc + lax.dot_general(lhs, rhs, NT, preferred_element_type=F32)
    grad_ref[...] = weigh(lw_ref[...], acc.T)


def final_kernel(rows, keep_ref, *refs):
    *got_refs, rw_ref, grad_ref, normed_ref, recip_ref, presence_ref, out_far, flat, staged, sent = refs
    hidden = rw_ref.shape[0]
    depth = keep_ref.shape[1] // hidden
    total = keep_ref[...]
    for got_ref in got_refs:
        total = total + got_ref[...].astype(F32)
    for e in range(hidden):
        flat[pl.ds(e, rows, stride=hidden), :] = total[:, e * depth : (e + 1) * depth]
    part = rows // 2
    copies = []
    for h in range(2):
        lanes = slice(h * part * depth, (h + 1) * part * depth)
        right = jnp.concatenate(
            [flat[j * hidden : (j + 1) * hidden, :] for j in range(h * part, (h + 1) * part)], axis=1
        )
        grad = (weigh(rw_ref[...], right) + grad_ref[:, lanes]) * presence_ref[:, lanes]
        normed = normed_ref[:, lanes]
        mean = jnp.mean(grad, axis=0, keepdims=True)
        cross = jnp.mean(grad * normed, axis=0, keepdims=True)
        out = (recip_ref[:, lanes] * (grad - mean - normed * cross)).T
        for i in range(part):
            staged[h, :, i, :] = out[i * depth : (i + 1) * depth, :]
        copies.append(
            pltpu.make_async_copy(staged.at[h], out_far.at[:, h * part : (h + 1) * part, :], sent.at[h])
        )
        copies[-1].start()
    for copy in copies:
        copy.wait()


def near_shape(dims, dtype):
    return pltpu.VMEM(dims, dtype)


def near(value):
    return pltpu.with_memory_space_constraint(value, pltpu.VMEM)


def far(value):
    return pltpu.with_memory_space_constraint(value, pltpu.HBM)


def call(kernel, name, out_shape, args, scratch=(), flops=0, in_specs=None, out_specs=None):
    vmem = pl.BlockSpec(memory_space=pltpu.VMEM)
    out_specs = out_specs or ((vmem,) * len(out_shape) if isinstance(out_shape, tuple) else vmem)
    return pl.pallas_call(
        kernel,
        out_shape=out_shape,
        in_specs=in_specs or [vmem] * len(args),
        out_specs=out_specs,
        scratch_shapes=scratch,
        compiler_params=PARAMS,
        cost_estimate=pl.CostEstimate(flops=flops, bytes_accessed=1 << 20, transcendentals=0),
        name=name,
    )(*args)


def shards(size, x, mask, residue_mask, lw, rw, ow, g):
    depth, rows, channels = x.shape
    hidden = lw.shape[1]
    width, pair = g.shape[1:]
    count = depth * rows
    flat_width = depth * hidden

    def exchange(value, bit):
        return lax.ppermute(value, "row", [(d, d ^ bit) for d in range(size)])

    sources = (x.reshape(count, channels), mask, residue_mask.reshape(1, width), lw.T, rw.T, ow, g)
    left, right, x, presence, lw, rw, owp, stack, inverse, g, repeat, diagonal = call(
        functools.partial(project_kernel, rows),
        "project",
        (
            near_shape((hidden, count), BF16),
            near_shape((rows, flat_width), BF16),
            near_shape((count, channels), BF16),
            near_shape((1, count), F32),
            near_shape((hidden, channels), BF16),
            near_shape((hidden, channels), BF16),
            near_shape(ow.shape, BF16),
            near_shape((ow.shape[0] // 256 * pair, 256), BF16),
            near_shape((width, rows), F32),
            near_shape(g.shape, BF16),
            near_shape((128, 128 // depth * 256), BF16),
            near_shape((256, 256), BF16),
        ),
        [far(v) for v in sources],
        [
            pltpu.VMEM(mask.shape, mask.dtype),
            pltpu.VMEM((1, width), residue_mask.dtype),
            pltpu.VMEM(ow.shape, BF16),
            pltpu.VMEM((count, channels), F32),
            pltpu.VMEM((rows * hidden, depth), F32),
            pltpu.VMEM(ow.shape, F32),
            pltpu.VMEM((width, rows), BF16),
            pltpu.VMEM((rows, count), BF16),
            pltpu.SemaphoreType.DMA((len(sources),)),
        ],
        in_specs=[pl.BlockSpec(memory_space=pl.ANY)] * len(sources),
    )
    bits = [1 << t for t in range(size.bit_length() - 1)]
    stages = [bits[t : t + 2] for t in range(1, len(bits), 2)]

    def partners(stage):
        found = [0]
        for bit in reversed(stage):
            found = found + [bit ^ f for f in found]
        return found

    def parts(total, stage):
        return [piece.astype(BF16) for piece in jnp.split(total, 1 << len(stage))]

    block = right
    for stage in stages[:0:-1]:
        block = [block] + [exchange(block, other) for other in partners(stage)[1:]]
        block = jnp.concatenate(block, axis=0)
    scaled, spread = call(
        functools.partial(spread_kernel, rows, size),
        "spread",
        (near_shape((width, rows * pair), BF16), near_shape((rows * pair, flat_width), BF16)),
        [near(v) for v in (g, inverse, left, stack, repeat, diagonal)],
        flops=2 * 2**30,
    )
    send = call(
        send_kernel,
        "send",
        near_shape((width // 2, flat_width), BF16),
        [near(scaled), near(spread)],
        flops=2**30,
    )
    scaled_again, send, block = lax.optimization_barrier((scaled, send, block))
    got = exchange(send, bits[0])
    keep, normed, recip = call(
        functools.partial(keep_kernel, rows),
        "keep",
        (
            near_shape((width // 2, flat_width), F32),
            near_shape((channels, count), F32),
            near_shape((1, count), F32),
        ),
        [near(v) for v in (scaled_again, spread, x)],
        [pltpu.VMEM((count, channels), F32)],
        flops=2**30,
    )
    total = keep + got.astype(F32)
    sums = parts(total, stages[0])
    joint = [
        exchange(jnp.concatenate([piece, block], axis=0), other) for piece, other in zip(sums[1:], partners(stages[0])[1:])
    ]
    cut = sums[0].shape[0]
    keep = total[:cut]
    for v in joint[::-1]:
        keep = lax.optimization_barrier(keep + v[:cut].astype(F32))
    joint, _ = lax.optimization_barrier((joint, keep))
    near_block = jnp.concatenate([block] + [v[cut:] for v in joint], axis=0)
    far_block = exchange(near_block, bits[0])
    got = []
    for stage in stages[1:]:
        total = keep + sum(v.astype(F32) for v in got) if got else keep
        sums = parts(total, stage)
        keep = total[: sums[0].shape[0]]
        got = [exchange(piece, other) for piece, other in zip(sums[1:], partners(stage)[1:])]
    outer = call(
        functools.partial(outer_kernel, rows),
        "outer",
        near_shape((hidden, count, pair), BF16),
        [near(v) for v in (near_block, far_block, scaled)],
        [pltpu.VMEM((flat_width, width), BF16)],
        flops=2**26,
    )
    grad = call(
        left_kernel,
        "left",
        near_shape((channels, count), F32),
        [near(v) for v in (outer, owp, lw)],
        flops=2**26,
    )
    out = call(
        functools.partial(final_kernel, rows),
        "final",
        jax.ShapeDtypeStruct((depth, rows, channels), F32),
        [near(v) for v in (keep, *got, rw, grad, normed, recip, presence)],
        [
            pltpu.VMEM((rows * hidden, depth), F32),
            pltpu.VMEM((2, depth, rows // 2, channels), F32),
            pltpu.SemaphoreType.DMA((2,)),
        ],
        out_specs=pl.BlockSpec(memory_space=pl.ANY),
    )
    return out


def solution(mesh):
    return jax.shard_map(
        functools.partial(shards, mesh.shape["row"]),
        mesh=mesh,
        in_specs=(
            P("groups", "row", None),
            P("groups", None),
            P("groups"),
            P(),
            P(),
            P(),
            P(("groups", "row"), None, None),
        ),
        out_specs=P("groups", "row", None),
        check_vma=False,
    )
```
